256 devices in a mesh: expert: 32 (over z, x), tensor: 8 (over y, core).
Axes of the slice: x: 4, y: 4, z: 8, core: 2. Of those that a mesh axis runs over, the one named last changes fastest.
Arguments:
- tokens: bfloat16 [4096, 4096], P('expert', 'tensor'), may hold values from -6 to 6
- expert_ids: int32 [4096, 8], P('expert'), may hold values from 0 to 63, all different within a row; in each aligned block of 128 rows (0 to 127, 128 to 255, ...) at most 24 rows name the same one
- combine_weight: float32 [4096, 8], P('expert'), may hold values from 0.05 to 0.5
- gate_weight: bfloat16 [64, 4096, 1024], P('expert', 'tensor'), may hold values from -0.09375 to 0.09375
- up_weight: bfloat16 [64, 4096, 1024], P('expert', 'tensor'), may hold values from -0.09375 to 0.09375
- down_weight: bfloat16 [64, 1024, 4096], P('expert', None, 'tensor'), may hold values from -0.1875 to 0.1875
- out_cotangent: bfloat16 [4096, 4096], P('expert', 'tensor'), may hold values from -3 to 3
Outputs:
- mixed: bfloat16 [4096, 4096], P('expert', 'tensor')
- token_grad: bfloat16 [4096, 4096], P('expert', 'tensor')
- combine_grad: float32 [4096, 8], P('expert')
- gate_grad: bfloat16 [64, 4096, 1024], P('expert', 'tensor')
- up_grad: bfloat16 [64, 4096, 1024], P('expert', 'tensor')
- down_grad: bfloat16 [64, 1024, 4096], P('expert', None, 'tensor')
The draws below stay inside these ranges and needn't reach their ends.
Inputs may be any that keep to these rules, and one draw needn't show every extreme that they name: `expert_ids`: each row names 8 different experts. Among the rows of one device no expert is named by more than 24 rows, a bound that some block reaches.
All inputs are finite; a program needn't handle non-finite values.
Results may differ from the reference program's by a relative error of at most 0.023.
Values may be sent and summed in bfloat16 or wider, within the bound.
No kernel may reach another device: no remote copies, remote signals or barrier semaphores. Data moves between devices by JAX's collectives and lax.ppermute only.
A program may use at most 128 MiB of HBM per device.

```python
import math
import jax
import jax.numpy as jnp
import numpy as np
from jax import lax

D = 4096
EXPERT_HIDDEN = 1024
TOP = 8
TOK_DEV = 128
EXPERTS = 64
TOKENS = 4096
CAP = 24
N_EXPERT = 32
N_TENSOR = 8


def levels(own_key, extent, split, low, top_value):
    def one(axis_at, parts):
        steps = jax.random.uniform(jax.random.fold_in(jax.random.fold_in(own_key, 6), axis_at), (parts,), jnp.float32, low / len(split), top_value / len(split))
        return jnp.repeat(jnp.exp(steps), extent[axis_at] // parts).reshape((-1,) + (1,) * (len(extent) - axis_at - 1))

    factor_of = one(*split[0])
    for cut in split[1:]:
        factor_of = factor_of * one(*cut)
    return factor_of


def routed_block(stream_key, own, number, rows, number_of, top, most, slope):
    order = jax.random.permutation(stream_key, number_of)
    packed, common = shares(number_of, rows * top, most, slope, True), shares(number_of, rows * top, most, slope, False)
    places = jnp.arange(number_of)

    def named(lengths, rotation):
        used = int((lengths > 0).sum())
        fixed = max(1, used // 4)
        shifted = fixed + (places - fixed + rotation * (used - fixed)) % max(1, number_of - fixed)
        return jnp.zeros((number_of,), jnp.int32).at[order[jnp.where(places < fixed, places, shifted)]].set(jnp.asarray(lengths, jnp.int32))

    lengths = jnp.where(number % 4 == 0, named(packed, number // 4), named(common, number - number // 4 - 1))
    mixed = jax.random.permutation(jax.random.fold_in(own, 3), number_of)
    source_of, receiver = mixed[0:number_of // 2 * 2:2], mixed[1:number_of // 2 * 2:2]
    margin = jnp.minimum(lengths[source_of] - 1, most - lengths[receiver]) // 2
    margin = jnp.where((source_of == order[0]) | (receiver == order[0]) | (lengths[receiver] == 0), 0, jnp.maximum(margin, 0))
    shifted = jax.random.randint(jax.random.fold_in(own, 4), (number_of // 2,), 0, 1 << 20) % (margin + 1)
    lengths = lengths.at[source_of].add(-shifted).at[receiver].add(shifted)
    labels = jnp.searchsorted(jnp.cumsum(lengths), jnp.arange(rows * top), side="right").astype(jnp.int32)
    table = labels.reshape(top, rows).T
    table = table[jax.random.permutation(jax.random.fold_in(own, 1), rows)]
    rotation = jax.random.randint(jax.random.fold_in(own, 2), (rows, 1), 0, top)
    return jnp.take_along_axis(table, (jnp.arange(top)[None, :] + rotation) % top, axis=1)


def shares(count, total, bound, slope, full):
    weights = [(1 << 20) // math.isqrt(rank ** slope) + 1 for rank in range(1, count + 1)]
    largest = bound if full else min(bound, max(-(-total // count), total * weights[0] // sum(weights)))
    least = 1 if total - largest >= count - 1 else 0
    given, spare = [largest] + [least] * (count - 1), total - largest - least * (count - 1)
    while spare > 0:
        candidates = [i for i in range(1, count) if given[i] < largest] or [i for i in range(1, count) if given[i] < bound]
        whole, budget = sum([weights[i] for i in candidates]), spare
        for i in candidates:
            extra = min(bound - given[i], max(1, budget * weights[i] // whole), spare)
            given[i] = given[i] + extra
            spare = spare - extra
    return np.array(given)


def centred(key, dims, spread, reach, shards=(), kind=jnp.bfloat16):
    result = jax.random.normal(key, dims, jnp.float32) * spread
    if len(shards) > 0:
        result = levels(key, dims, shards, -0.22, 0.18) * result
    return jnp.clip(result, min=-reach, max=reach).astype(kind)


def setup_inputs(seed: int = 0) -> dict:
    arg_keys = jax.random.split(jax.random.key(seed), 8)
    tokens = centred(arg_keys[0], (TOKENS, D), 1.0, 6.0, ((0, 32), (1, 8)))
    expert_ids_keys = jax.random.split(jax.random.fold_in(arg_keys[1], 1), TOKENS // TOK_DEV)
    expert_ids_turns = jax.random.permutation(jax.random.fold_in(arg_keys[1], 3), TOKENS // TOK_DEV)
    expert_ids = jax.vmap(lambda own, number: routed_block(jax.random.fold_in(arg_keys[1], 2), own, number, TOK_DEV, EXPERTS, TOP, CAP, 2))(expert_ids_keys, expert_ids_turns).reshape((TOKENS, TOP))
    combine_weight = jnp.clip(jnp.exp(math.log(0.5) - 2.3025851 * jax.random.uniform(arg_keys[2], (TOKENS, TOP), jnp.float32) ** levels(arg_keys[2], (TOKENS, TOP), ((0, 32),), -0.2, 0.2)), 0.05, 0.5)
    gate_weight = centred(arg_keys[3], (EXPERTS, D, EXPERT_HIDDEN), D ** -0.5, 0.09375, ((0, 32), (1, 8)))
    up_weight = centred(arg_keys[4], (EXPERTS, D, EXPERT_HIDDEN), D ** -0.5, 0.09375, ((0, 32), (1, 8)))
    down_weight = centred(arg_keys[5], (EXPERTS, EXPERT_HIDDEN, D), EXPERT_HIDDEN ** -0.5, 0.1875, ((0, 32), (2, 8)))
    out_cotangent = centred(arg_keys[6], (TOKENS, D), 0.5, 3.0, ((0, 32), (1, 8)))
    return {"tokens": tokens, "expert_ids": expert_ids, "combine_weight": combine_weight, "gate_weight": gate_weight, "up_weight": up_weight, "down_weight": down_weight, "out_cotangent": out_cotangent}


def rounded(value):
    return lax.optimization_barrier(value.astype(jnp.bfloat16)).astype(jnp.float32)


def block_total_sum(left, right_blocks, form):
    return jnp.sum(rounded(jnp.einsum(form, left, right_blocks, precision=lax.Precision.HIGHEST)), axis=0)


def reference(tokens, expert_ids, combine_weight, gate_weight, up_weight, down_weight, out_cotangent):
    pair_block = TOK_DEV * TOP
    pair_total = TOKENS * TOP
    capacity_slot_rows = N_EXPERT * CAP
    partial_share = D // N_TENSOR
    block_ids = expert_ids.reshape(N_EXPERT, pair_block)
    onehot = (block_ids[:, :, None] == jnp.arange(EXPERTS, dtype=jnp.int32)[None, None, :]).astype(jnp.int32)
    position = jnp.sum(jnp.cumsum(onehot, axis=1) * onehot, axis=2) - 1
    row_within = jnp.arange(N_EXPERT, dtype=jnp.int32)[:, None] * CAP + position
    pair_index = jnp.arange(pair_total, dtype=jnp.int32)
    table = jnp.full((EXPERTS, capacity_slot_rows), pair_total, jnp.int32)
    table = table.at[expert_ids.reshape(pair_total), row_within.reshape(pair_total).astype(jnp.int32)].set(pair_index)
    flat_weight = combine_weight.reshape(pair_total).astype(jnp.float32)
    cotangent = out_cotangent.astype(jnp.float32)
    highest = lax.Precision.HIGHEST

    def per_expert(carry, inputs):
        mixed_acc, grad_acc, combine_acc = carry
        rows, gate_w, up_w, down_w = inputs
        filled = rows < pair_total
        safe = jnp.minimum(rows, pair_total - 1)
        token_of = safe // TOP
        weight = jnp.where(filled, flat_weight[safe], jnp.float32(0.0))
        routed = jnp.where(filled[:, None], tokens[token_of].astype(jnp.float32), jnp.float32(0.0))
        incoming_gradient = rounded(weight[:, None] * cotangent[token_of])
        gate_matrix_float = gate_w.astype(jnp.float32)
        up_matrix_float = up_w.astype(jnp.float32)
        down_matrix_float = down_w.astype(jnp.float32)
        dispatched_blocks = routed.reshape(capacity_slot_rows, N_TENSOR, partial_share)
        gate_matrix = block_total_sum(dispatched_blocks, gate_matrix_float.reshape(N_TENSOR, partial_share, EXPERT_HIDDEN), "oem,eml->eol")
        up_matrix = block_total_sum(dispatched_blocks, up_matrix_float.reshape(N_TENSOR, partial_share, EXPERT_HIDDEN), "oem,eml->eol")
        hidden_act = rounded(jax.nn.silu(gate_matrix) * up_matrix)
        expert_out = rounded(jnp.dot(hidden_act, down_matrix_float, precision=highest))
        hidden_state_cotangent = block_total_sum(incoming_gradient.reshape(capacity_slot_rows, N_TENSOR, partial_share), down_matrix_float.reshape(EXPERT_HIDDEN, N_TENSOR, partial_share), "elb,glb->leg")
        down_grad = jnp.dot(hidden_act.T, incoming_gradient, precision=highest).astype(jnp.bfloat16)
        sigma = jax.nn.sigmoid(gate_matrix)
        gate_diff = rounded(hidden_state_cotangent * up_matrix * sigma * (1.0 + gate_matrix * (1.0 - sigma)))
        up_diff = rounded(hidden_state_cotangent * jax.nn.silu(gate_matrix))
        routed_grad = rounded(jnp.dot(gate_diff, gate_matrix_float.T, precision=highest) + jnp.dot(up_diff, up_matrix_float.T, precision=highest))
        gate_grad = jnp.dot(routed.T, gate_diff, precision=highest).astype(jnp.bfloat16)
        up_grad = jnp.dot(routed.T, up_diff, precision=highest).astype(jnp.bfloat16)
        mixed_acc = mixed_acc.at[token_of].add(weight[:, None] * expert_out)
        grad_acc = grad_acc.at[token_of].add(routed_grad)
        pair_dot = jnp.where(filled, jnp.sum(cotangent[token_of] * expert_out, axis=1), jnp.float32(0.0))
        combine_acc = combine_acc.at[safe].add(pair_dot)
        return (mixed_acc, grad_acc, combine_acc), (gate_grad, up_grad, down_grad)

    start_carry = (jnp.zeros((TOKENS, D), jnp.float32), jnp.zeros((TOKENS, D), jnp.float32), jnp.zeros((pair_total,), jnp.float32))
    final, grads = lax.scan(per_expert, start_carry, (table, gate_weight, up_weight, down_weight))
    mixed_acc, grad_acc, combine_acc = final
    gate_grads, up_grads, down_grads = grads
    return (mixed_acc.astype(jnp.bfloat16), grad_acc.astype(jnp.bfloat16), combine_acc.reshape(TOKENS, TOP), gate_grads, up_grads, down_grads)
```

```python
import jax
import jax.numpy as jnp
from jax import lax
from jax.experimental import pallas as pl
from jax.experimental.pallas import tpu as pltpu
from jax.sharding import PartitionSpec as P

NZ, NX, NY = 8, 4, 4
CHUNKS = ((0, 1, 7, 2), (6, 3, 5, 4))
LANES = 128
F32, BF16 = jnp.float32, jnp.bfloat16


def z_shift(k):
    return [(z * NX + x, (z + k) % NZ * NX + x) for z in range(NZ) for x in range(NX)]


def x_shift(k):
    return [(z * NX + x, z * NX + (x + k) % NX) for z in range(NZ) for x in range(NX)]


def y_shift(k):
    return [(y * 2 + c, (y + k) % NY * 2 + c) for y in range(NY) for c in range(2)]


def flip(mask):
    return [(i, i ^ mask) for i in range(NY * 2)]


def call(body, pos, grid, ins, outs, scratch=(), flops=0):
    arrays = [a for a, _ in ins]
    moved = sum(a.size * a.dtype.itemsize for a in arrays) + sum(
        s.size * s.dtype.itemsize for s, _ in outs
    )
    return pl.pallas_call(
        body,
        out_shape=[s for s, _ in outs],
        grid_spec=pltpu.PrefetchScalarGridSpec(
            num_scalar_prefetch=1,
            grid=grid,
            in_specs=[s for _, s in ins],
            out_specs=[s for _, s in outs],
            scratch_shapes=list(scratch),
        ),
        compiler_params=pltpu.CompilerParams(vmem_limit_bytes=40 << 20),
        cost_estimate=pl.CostEstimate(flops=flops, bytes_accessed=moved, transcendentals=0),
    )(pos, *arrays)


def whole(shape):
    return pl.BlockSpec(shape, lambda i, pos: (0,) * len(shape))


def sds(shape, dtype=BF16):
    return jax.ShapeDtypeStruct(shape, dtype)


def dot(a, b, ca, cb):
    return lax.dot_general(a, b, (((ca,), (cb,)), ((), ())), preferred_element_type=F32)


def triangle():
    rows = lax.broadcasted_iota(jnp.int32, (LANES, LANES), 0)
    cols = lax.broadcasted_iota(jnp.int32, (LANES, LANES), 1)
    return jnp.where(rows < cols, 1.0, 0.0).astype(BF16)


def slots(meta, pos, cap):
    ids = meta[:8, :LANES]
    weight = meta[:8, LANES : 2 * LANES] + meta[:8, 2 * LANES : 3 * LANES] + meta[:8, 3 * LANES :]
    named, weights = [], []
    for k in range(NX):
        for e in range(2):
            expert = (pos[0] * NX + lax.rem(pos[1] + k, NX)) * 2 + e
            hit = ids == expert.astype(F32)
            named.append(jnp.sum(jnp.where(hit, 1.0, 0.0), axis=0, keepdims=True))
            weights.append(jnp.sum(jnp.where(hit, weight, 0.0), axis=0, keepdims=True))
    all_named = jnp.concatenate(named, axis=0)
    place = dot(all_named.astype(BF16), triangle(), 1, 0)
    place = jnp.where(all_named > 0.5, place, -1.0)
    count = lax.broadcasted_iota(jnp.int32, (cap, LANES), 0).astype(F32)
    tables = [jnp.where(count == place[q : q + 1], 1.0, 0.0) for q in range(2 * NX)]
    return tables, weights


def dispatch(pos, metas, blocks, cap, weighted):
    n, width = len(metas), blocks[0].shape[1]

    def body(pos_ref, *refs):
        p = (pos_ref[0], pos_ref[1])
        rows = []
        for i in range(n):
            tables, weights = slots(refs[i][...].astype(F32), p, cap)
            table = jnp.concatenate(tables, axis=0)
            taken = dot(table.astype(BF16), refs[n + i][...], 1, 0)
            if weighted:
                scale = jnp.concatenate(
                    [jnp.sum(t * w, axis=1, keepdims=True) for t, w in zip(tables, weights)], axis=0
                )
                taken = taken * scale
            rows.append(taken)
        for k in range(NX):
            for e in range(2):
                at = (k * 2 + e) * cap
                refs[2 * n + k][e] = jnp.concatenate(
                    [r[at : at + cap] for r in rows], axis=0
                ).astype(BF16)

    meta_spec = pl.BlockSpec((16, 4 * LANES), lambda i, pos: (0, 0))
    if metas[0].shape[0] > 16:
        meta_spec = pl.BlockSpec((16, 4 * LANES), lambda i, pos: (LANES // 16, 0))
    ins = [(m, meta_spec) for m in metas] + [(b, whole((LANES, width))) for b in blocks]
    piece = (2, n * cap, width)
    outs = [(sds(piece), whole(piece)) for _ in range(NX)]
    return call(body, pos, (1,), ins, outs, flops=4 * n * NX * cap * LANES * width)


def combine(pos, metas, pieces, cots, offsets, cap):
    n, width = len(metas), pieces[0].shape[2]
    mixing = cots is not None

    def body(pos_ref, *refs):
        p = (pos_ref[0], pos_ref[1])
        pieces_in = refs[n : n + NX]
        cots_in = refs[n + NX : n + NX + n] if mixing else ()
        outs = refs[len(refs) - n :]
        wide = [[pieces_in[k][e].astype(F32) for e in range(2)] for k in range(NX)]
        for i in range(n):
            tables, weights = slots(refs[i][...].astype(F32), p, cap)
            table = jnp.concatenate(tables, axis=0)
            rows = jnp.concatenate(
                [wide[k][e][i * cap : (i + 1) * cap] for k in range(NX) for e in range(2)], axis=0
            )
            rows16 = rows.astype(BF16)
            if mixing:
                scaled = jnp.concatenate([t * w for t, w in zip(tables, weights)], axis=0)
                high = scaled.astype(BF16)
                low = (scaled - high.astype(F32)).astype(BF16)
                total = dot(high, rows16, 0, 0) + dot(low, rows16, 0, 0)
                picked = dot(table.astype(BF16), cots_in[i][...], 1, 0)
                each = jnp.sum(picked * rows, axis=1, keepdims=True)
                grads = jnp.concatenate(
                    [
                        jnp.sum(t * each[q * cap : (q + 1) * cap], axis=0, keepdims=True)
                        for q, t in enumerate(tables)
                    ]
                    + [jnp.zeros((8 - 2 * NX, LANES), F32)] * (2 * NX < 8),
                    axis=0,
                )
            else:
                total = dot(table.astype(BF16), rows16, 0, 0)
            if offsets[i] == 0:
                outs[i][0:LANES, :] = total
                if mixing:
                    outs[i][LANES : LANES + 8, 0:LANES] = grads
            else:
                outs[i][0:LANES, :] = total.astype(BF16)
                if mixing:
                    top = grads.astype(BF16)
                    outs[i][LANES : LANES + 16, :] = jnp.zeros((16, width), BF16)
                    outs[i][LANES : LANES + 16, 0:LANES] = jnp.concatenate(
                        [top.astype(F32), grads - top.astype(F32)], axis=0
                    ).astype(BF16)

    meta_spec = pl.BlockSpec((16, 4 * LANES), lambda i, pos: (0, 0))
    if metas[0].shape[0] > 16:
        meta_spec = pl.BlockSpec((16, 4 * LANES), lambda i, pos: (LANES // 16, 0))
    ins = [(m, meta_spec) for m in metas]
    ins += [(q, whole(q.shape)) for q in pieces]
    if mixing:
        ins += [(b, whole(b.shape)) for b in cots]
    outs = []
    for j in offsets:
        if j == 0:
            shape, kind = (LANES + 8 * mixing, width), F32
        else:
            shape, kind = (LANES + 16 * mixing, width), BF16
        outs.append((sds(shape, kind), whole(shape)))
    return call(body, pos, (1,), ins, outs, flops=12 * n * NX * cap * LANES * width)


def weight_spec(w, across, other):
    rows, cols = w.shape[1], w.shape[2]
    half = (lambda pos: 1 - pos[3]) if other else (lambda pos: pos[3])
    if across:
        return pl.BlockSpec((1, rows // 2, cols), lambda e, pos: (e, half(pos), 0))
    return pl.BlockSpec((1, rows, cols // 2), lambda e, pos: (e, 0, half(pos)))


def partial_other(pos, pieces, mats, across):
    m, (_, part, width) = len(mats), pieces[0].shape
    rows = NX * part

    def body(pos_ref, *refs):
        ins, weights, (theirs, joined) = refs[:NX], refs[NX : NX + m], refs[NX + m :]
        left = jnp.concatenate([r[0] for r in ins], axis=0)
        joined[0] = left
        for i in range(m):
            out = dot(left, weights[i][0], 1, 1 if across else 0).astype(BF16)
            for y in range(NY):
                theirs[y, i, 0] = out[:, y * LANES : (y + 1) * LANES]

    ins = [(p, pl.BlockSpec((1, part, width), lambda e, pos: (e, 0, 0))) for p in pieces]
    ins += [(w, weight_spec(w, across, True)) for w in mats]
    outs = [
        (
            sds((NY, m, 2, rows, LANES)),
            pl.BlockSpec((NY, m, 1, rows, LANES), lambda e, pos: (0, 0, e, 0, 0)),
        ),
        (sds((2, rows, width)), pl.BlockSpec((1, rows, width), lambda e, pos: (e, 0, 0))),
    ]
    return call(body, pos, (2,), ins, outs, flops=4 * m * rows * width * NY * LANES)


def partial_own(pos, joined, mats, got, across):
    m, (_, rows, width) = len(mats), joined.shape

    def body(pos_ref, joined_ref, *refs):
        weights, got_ref, outs, hold = refs[:m], refs[m], refs[m + 1 : -1], refs[-1]
        for i in range(m):
            out = dot(joined_ref[0], weights[i][0], 1, 1 if across else 0)
            for y in range(NY):
                hold[y, i] = out[:, y * LANES : (y + 1) * LANES]
        for k in range(NY):
            at = lax.rem(pos_ref[2] + k, NY)
            for i in range(m):
                outs[k][i, 0] = (hold[at, i] + got_ref[at, i, 0].astype(F32)).astype(BF16)

    ins = [(joined, pl.BlockSpec((1, rows, width), lambda e, pos: (e, 0, 0)))]
    ins += [(w, weight_spec(w, across, False)) for w in mats]
    ins += [
        (got, pl.BlockSpec((NY, m, 1, rows, LANES), lambda e, pos: (0, 0, e, 0, 0))),
    ]
    outs = [
        (sds((m, 2, rows, LANES)), pl.BlockSpec((m, 1, rows, LANES), lambda e, pos: (0, e, 0, 0)))
        for _ in range(NY)
    ]
    scratch = [pltpu.VMEM((NY, m, rows, LANES), F32)]
    return call(body, pos, (2,), ins, outs, scratch, flops=4 * m * rows * width * NY * LANES)


def reduced(pos, pieces, mats, across):
    theirs, joined = partial_other(pos, pieces, mats, across)
    got = lax.ppermute(theirs, "tensor", flip(1))
    parts = partial_own(pos, joined, mats, got, across)
    terms = [parts[0]] + [lax.ppermute(parts[k], "tensor", y_shift(k)) for k in (2, 1, 3)]
    return terms, joined


def term_sum(refs, i):
    total = refs[0][i, 0].astype(F32)
    for r in refs[1:]:
        total = total + r[i, 0].astype(F32)
    return total


def sigmoid(v):
    return 1.0 / (1.0 + jnp.exp(-v))


def term_specs(terms):
    m, _, rows, _ = terms[0].shape
    spec = pl.BlockSpec((m, 1, rows, LANES), lambda e, pos: (0, e, 0, 0))
    return [(t, spec) for t in terms]


def activated(pos, terms):
    rows = terms[0].shape[2]

    def body(pos_ref, *refs):
        gate, up = term_sum(refs[:NY], 0), term_sum(refs[:NY], 1)
        refs[NY][0] = (gate * sigmoid(gate) * up).astype(BF16)

    outs = [(sds((2, rows, LANES)), pl.BlockSpec((1, rows, LANES), lambda e, pos: (e, 0, 0)))]
    return call(body, pos, (2,), term_specs(terms), outs)[0]


def differed(pos, terms, hid_terms):
    rows = terms[0].shape[2]

    def body(pos_ref, *refs):
        gate, up = term_sum(refs[:NY], 0), term_sum(refs[:NY], 1)
        hid = term_sum(refs[NY : 2 * NY], 0)
        s = sigmoid(gate)
        refs[2 * NY][0, 0] = (hid * up * s * (1.0 + gate * (1.0 - s))).astype(BF16)
        refs[2 * NY][0, 1] = (hid * (gate * s)).astype(BF16)

    outs = [
        (
            sds((2, 2, rows, LANES)),
            pl.BlockSpec((1, 2, rows, LANES), lambda e, pos: (e, 0, 0, 0)),
        )
    ]
    return call(body, pos, (2,), term_specs(terms) + term_specs(hid_terms), outs)[0]


def gathered(own):
    before = lax.ppermute(own, "tensor", y_shift(1))
    after = lax.ppermute(own, "tensor", y_shift(-1))
    far0 = lax.ppermute(before[:1], "tensor", y_shift(1))
    far1 = lax.ppermute(after[1:], "tensor", y_shift(-1))
    mine = [own, before, after, far0, far1]
    return mine + [lax.ppermute(a, "tensor", flip(1)) for a in mine]


def products(pos, shares, mats, across, part):
    flat = len(mats) == 1
    rows = shares[0].shape[-2]
    m, hidden = len(mats), 2 * NY * LANES
    width = mats[0].shape[1] if across else mats[0].shape[2]

    def body(pos_ref, *refs):
        ins, weights = refs[:10], refs[10 : 10 + m]
        outs, fulls = refs[10 + m : 10 + m + NX], refs[10 + m + NX :]
        e, y, c = pl.program_id(0), pos_ref[2], pos_ref[3]
        total = None
        for i in range(m):
            for side in range(2):
                core = c if side == 0 else 1 - c
                group = ins[side * 5 : side * 5 + 5]
                read = [(g[0] if flat else g[0, i]) for g in group]
                for d, value in ((0, read[0]), (NY - 1, read[1]), (1, read[2])):
                    at = pl.multiple_of((core * NY + lax.rem(y + d, NY)) * LANES, LANES)
                    fulls[i][0, :, pl.ds(at, LANES)] = value
                at = pl.multiple_of((core * NY + lax.rem(y + 2, NY)) * LANES, LANES)

                @pl.when(e == 0)
                def _():
                    fulls[i][0, :, pl.ds(at, LANES)] = read[3]

                @pl.when(e == 1)
                def _():
                    fulls[i][0, :, pl.ds(at, LANES)] = read[4]

            term = dot(fulls[i][0], weights[i][0], 1, 1 if across else 0)
            total = term if total is None else total + term
        total = total.astype(BF16)
        for k in range(NX):
            outs[k][0] = total[k * part : (k + 1) * part]

    if flat:
        block = (1, rows, LANES)
        moving = pl.BlockSpec(block, lambda e, pos: (e, 0, 0))
        still = pl.BlockSpec(block, lambda e, pos: (0, 0, 0))
    else:
        block = (1, m, rows, LANES)
        moving = pl.BlockSpec(block, lambda e, pos: (e, 0, 0, 0))
        still = pl.BlockSpec(block, lambda e, pos: (0, 0, 0, 0))
    ins = [(s, still if i % 5 > 2 else moving) for i, s in enumerate(shares)]
    ins += [(w, pl.BlockSpec((1,) + w.shape[1:], lambda e, pos: (e, 0, 0))) for w in mats]
    outs = [
        (sds((2, part, width)), pl.BlockSpec((1, part, width), lambda e, pos: (e, 0, 0)))
        for _ in range(NX)
    ]
    outs += [
        (sds((2, rows, hidden)), pl.BlockSpec((1, rows, hidden), lambda e, pos: (e, 0, 0)))
        for _ in range(m)
    ]
    got = call(body, pos, (2,), ins, outs, flops=4 * m * rows * width * hidden)
    return got[:NX], got[NX:]


def weight_grad(pos, lefts, rights, left_wide):
    n = len(lefts)
    a, b = lefts[0].shape[2], rights[0].shape[2]
    ba, bb = (a // 2, b) if left_wide else (a, b // 2)

    def body(pos_ref, *refs):
        total = dot(refs[0][0], refs[n][0], 0, 0)
        for i in range(1, n):
            total = total + dot(refs[i][0], refs[n + i][0], 0, 0)
        refs[2 * n][0] = total.astype(BF16)

    def spec(v, size, cut):
        return pl.BlockSpec((1, v.shape[1], size), lambda e, h, pos: (e, 0, h if cut else 0))

    ins = [(v, spec(v, ba, left_wide)) for v in lefts]
    ins += [(v, spec(v, bb, not left_wide)) for v in rights]
    out = pl.BlockSpec(
        (1, ba, bb), lambda e, h, pos: (e, h if left_wide else 0, 0 if left_wide else h)
    )
    rows = sum(v.shape[1] for v in lefts)
    return call(body, pos, (2, 2), ins, [(sds((2, a, b)), out)], flops=4 * rows * a * b)[0]


def spread(pieces):
    return [pieces[0]] + [lax.ppermute(pieces[k], "expert", x_shift(k)) for k in range(1, NX)]


def unspread(pieces):
    return [pieces[0]] + [lax.ppermute(pieces[k], "expert", x_shift(-k)) for k in range(1, NX)]


def per_device(
    tokens, expert_ids, combine_weight, gate_weight, up_weight, down_weight, out_cotangent
):
    tok_rows, width = tokens.shape
    top_count = expert_ids.shape[1]
    cap = 3 * tok_rows * top_count // (2 * gate_weight.shape[0] * NZ * NX)
    group, share = lax.axis_index("expert"), lax.axis_index("tensor")
    pos = jnp.stack([group // NX, group % NX, share // 2, share % 2]).astype(jnp.int32)

    ids = expert_ids.T
    weight = combine_weight.T
    high = lax.reduce_precision(weight, 8, 7)
    middle = lax.reduce_precision(weight - high, 8, 7)
    low = weight - high - middle
    meta = jnp.concatenate([ids.astype(F32), high, middle, low], axis=1).astype(BF16)
    meta = jnp.pad(meta, ((0, 8), (0, 0)))
    if width == 4 * LANES:
        sent = jnp.concatenate([tokens, meta], axis=0)
        tok_of = {0: sent}
        for j in sum(CHUNKS, ()):
            if j:
                tok_of[j] = lax.ppermute(sent, "expert", z_shift(j))
        meta_of = tok_of
    else:
        tok_of, meta_of = {0: tokens}, {0: meta}
        for j in range(1, NZ):
            tok_of[j] = lax.ppermute(tokens, "expert", z_shift(j))
            meta_of[j] = lax.ppermute(meta, "expert", z_shift(j))
    cot_of = {0: out_cotangent}
    for j in sum(CHUNKS, ()):
        if j:
            cot_of[j] = lax.ppermute(out_cotangent, "expert", z_shift(j))

    mixed_parts, grad_parts = {}, {}
    routed, cotangents, acts, gates, ups = [], [], [], [], []
    for offsets in CHUNKS:
        metas = [meta_of[j] for j in offsets]
        toks, cots = [tok_of[j] for j in offsets], [cot_of[j] for j in offsets]
        part = len(offsets) * cap
        terms, rows = reduced(
            pos, spread(dispatch(pos, metas, toks, cap, False)), [gate_weight, up_weight], False
        )
        routed.append(rows)
        hid_terms, rows = reduced(
            pos, spread(dispatch(pos, metas, cots, cap, True)), [down_weight], True
        )
        cotangents.append(rows)
        out_pieces, full = products(
            pos, gathered(activated(pos, terms)), [down_weight], False, part
        )
        acts.append(full[0])
        parts = combine(pos, metas, unspread(out_pieces), cots, offsets, cap)
        for j, value in zip(offsets, parts):
            mixed_parts[j] = value if j == 0 else lax.ppermute(value, "expert", z_shift(-j))
        grad_pieces, full = products(
            pos, gathered(differed(pos, terms, hid_terms)), [gate_weight, up_weight], True, part
        )
        gates.append(full[0])
        ups.append(full[1])
        parts = combine(pos, metas, unspread(grad_pieces), None, offsets, cap)
        for j, value in zip(offsets, parts):
            grad_parts[j] = value if j == 0 else lax.ppermute(value, "expert", z_shift(-j))

    mixed = sum(mixed_parts[j][:tok_rows].astype(F32) for j in range(NZ)).astype(BF16)
    token_grad = sum(grad_parts[j].astype(F32) for j in range(NZ)).astype(BF16)

    grads = jnp.zeros(ids.shape, F32)
    for j in range(NZ):
        table = mixed_parts[j][tok_rows : tok_rows + 8, :LANES].astype(F32)
        if j:
            table = table + mixed_parts[j][tok_rows + 8 :, :LANES].astype(F32)
        for k in range(NX):
            for e in range(2):
                expert = ((pos[0] + j) % NZ * NX + (pos[1] + k) % NX) * 2 + e
                grads = grads + jnp.where(ids == expert, table[k * 2 + e][None, :], 0.0)
    for mask in (1, 2, 4):
        grads = grads + lax.ppermute(grads, "tensor", flip(mask))

    gate_grad = weight_grad(pos, routed, gates, False)
    up_grad = weight_grad(pos, routed, ups, False)
    down_grad = weight_grad(pos, acts, cotangents, True)
    return (mixed, token_grad, grads.T, gate_grad, up_grad, down_grad)


def solution(mesh):
    placed = (
        P("expert", "tensor"),
        P("expert", None),
        P("expert", None),
        P("expert", "tensor", None),
        P("expert", "tensor", None),
        P("expert", None, "tensor"),
        P("expert", "tensor"),
    )
    return jax.shard_map(
        per_device,
        mesh=mesh,
        in_specs=placed,
        out_specs=(
            P("expert", "tensor"),
            P("expert", "tensor"),
            P("expert", None),
            P("expert", "tensor", None),
            P("expert", "tensor", None),
            P("expert", None, "tensor"),
        ),
        check_vma=False,
    )
```

```python
import jax
import jax.numpy as jnp
from jax import lax
from jax.experimental import pallas as pl
from jax.experimental.pallas import tpu as pltpu
from jax.sharding import PartitionSpec as P

NZ, NX, NY = 8, 4, 4
CHUNKS = ((0, 1, 7, 2), (6, 3, 5, 4))
LANES = 128
F32, BF16 = jnp.float32, jnp.bfloat16


def z_shift(k):
    return [(z * NX + x, (z + k) % NZ * NX + x) for z in range(NZ) for x in range(NX)]


def x_shift(k):
    return [(z * NX + x, z * NX + (x + k) % NX) for z in range(NZ) for x in range(NX)]


def y_shift(k):
    return [(y * 2 + c, (y + k) % NY * 2 + c) for y in range(NY) for c in range(2)]


def flip(mask):
    return [(i, i ^ mask) for i in range(NY * 2)]


def call(body, pos, grid, ins, outs, scratch=(), flops=0):
    arrays = [a for a, _ in ins]
    moved = sum(a.size * a.dtype.itemsize for a in arrays) + sum(
        s.size * s.dtype.itemsize for s, _ in outs
    )
    return pl.pallas_call(
        body,
        out_shape=[s for s, _ in outs],
        grid_spec=pltpu.PrefetchScalarGridSpec(
            num_scalar_prefetch=1,
            grid=grid,
            in_specs=[s for _, s in ins],
            out_specs=[s for _, s in outs],
            scratch_shapes=list(scratch),
        ),
        compiler_params=pltpu.CompilerParams(vmem_limit_bytes=56 << 20),
        cost_estimate=pl.CostEstimate(flops=flops, bytes_accessed=moved, transcendentals=0),
    )(pos, *arrays)


def whole(shape):
    return pl.BlockSpec(shape, lambda i, pos: (0,) * len(shape))


def sds(shape, dtype=BF16):
    return jax.ShapeDtypeStruct(shape, dtype)


def dot(a, b, ca, cb):
    return lax.dot_general(a, b, (((ca,), (cb,)), ((), ())), preferred_element_type=F32)


def triangle():
    rows = lax.broadcasted_iota(jnp.int32, (LANES, LANES), 0)
    cols = lax.broadcasted_iota(jnp.int32, (LANES, LANES), 1)
    return jnp.where(rows < cols, 1.0, 0.0).astype(BF16)


def slots(meta, pos, cap):
    ids = meta[:8, :LANES]
    weight = meta[:8, LANES : 2 * LANES] + meta[:8, 2 * LANES : 3 * LANES] + meta[:8, 3 * LANES :]
    named, weights = [], []
    for k in range(NX):
        for e in range(2):
            expert = (pos[0] * NX + lax.rem(pos[1] + k, NX)) * 2 + e
            hit = ids == expert.astype(F32)
            named.append(jnp.sum(jnp.where(hit, 1.0, 0.0), axis=0, keepdims=True))
            weights.append(jnp.sum(jnp.where(hit, weight, 0.0), axis=0, keepdims=True))
    all_named = jnp.concatenate(named, axis=0)
    place = dot(all_named.astype(BF16), triangle(), 1, 0)
    place = jnp.where(all_named > 0.5, place, -1.0)
    count = lax.broadcasted_iota(jnp.int32, (cap, LANES), 0).astype(F32)
    tables = [jnp.where(count == place[q : q + 1], 1.0, 0.0) for q in range(2 * NX)]
    return tables, weights


def dispatch(pos, blocks, cap):
    n, width = len(blocks), blocks[0].shape[1]
    half = width // 2

    def body(pos_ref, *refs):
        p = (pos_ref[0], pos_ref[1])
        rows = []
        for i in range(n):
            meta = refs[i][LANES : LANES + 16, 0 : 4 * LANES].astype(F32)
            tables, weights = slots(meta, p, cap)
            table = jnp.concatenate(tables, axis=0)
            taken = dot(table.astype(BF16), refs[i][0:LANES, :], 1, 0)
            scale = jnp.concatenate(
                [jnp.sum(t * w, axis=1, keepdims=True) for t, w in zip(tables, weights)], axis=0
            )
            rows.append((taken[:, :half], taken[:, half:] * scale))
        for k in range(NX):
            for e in range(2):
                at = (k * 2 + e) * cap
                for side in range(2):
                    refs[n + k][e, :, side * half : (side + 1) * half] = jnp.concatenate(
                        [r[side][at : at + cap] for r in rows], axis=0
                    ).astype(BF16)

    ins = [(b, whole(b.shape)) for b in blocks]
    piece = (2, n * cap, width)
    outs = [(sds(piece), whole(piece)) for _ in range(NX)]
    return call(body, pos, (1,), ins, outs, flops=4 * n * NX * cap * LANES * width)


def combine(pos, blocks, pieces, offsets, cap):
    n, width = len(blocks), pieces[0].shape[2]
    half = width // 2

    def body(pos_ref, *refs):
        p = (pos_ref[0], pos_ref[1])
        pieces_in, outs = refs[n : n + NX], refs[n + NX :]
        wide = [[pieces_in[k][e].astype(F32) for e in range(2)] for k in range(NX)]
        for i in range(n):
            meta = refs[i][LANES : LANES + 16, 0 : 4 * LANES].astype(F32)
            tables, weights = slots(meta, p, cap)
            table = jnp.concatenate(tables, axis=0).astype(BF16)
            rows = jnp.concatenate(
                [wide[k][e][i * cap : (i + 1) * cap] for k in range(NX) for e in range(2)], axis=0
            )
            rows16 = rows.astype(BF16)
            scaled = jnp.concatenate([t * w for t, w in zip(tables, weights)], axis=0)
            high = scaled.astype(BF16)
            low = (scaled - high.astype(F32)).astype(BF16)
            mixed = dot(high, rows16[:, :half], 0, 0) + dot(low, rows16[:, :half], 0, 0)
            back = dot(table, rows16[:, half:], 0, 0)
            picked = dot(table, refs[i][0:LANES, half:], 1, 0)
            each = jnp.sum(picked * rows[:, :half], axis=1, keepdims=True)
            grads = jnp.concatenate(
                [
                    jnp.sum(t * each[q * cap : (q + 1) * cap], axis=0, keepdims=True)
                    for q, t in enumerate(tables)
                ]
                + [jnp.zeros((8 - 2 * NX, LANES), F32)] * (2 * NX < 8),
                axis=0,
            )
            kind = F32 if offsets[i] == 0 else BF16
            outs[i][0:LANES, :half] = mixed.astype(kind)
            outs[i][0:LANES, half:] = back.astype(kind)
            if offsets[i] == 0:
                outs[i][LANES : LANES + 8, 0:LANES] = grads
            else:
                top = grads.astype(BF16).astype(F32)
                outs[i][LANES : LANES + 16, :] = jnp.zeros((16, width), BF16)
                outs[i][LANES : LANES + 16, 0:LANES] = jnp.concatenate(
                    [top, grads - top], axis=0
                ).astype(BF16)

    ins = [(b, whole(b.shape)) for b in blocks]
    ins += [(q, whole(q.shape)) for q in pieces]
    outs = []
    for j in offsets:
        shape, kind = ((LANES + 8, width), F32) if j == 0 else ((LANES + 16, width), BF16)
        outs.append((sds(shape, kind), whole(shape)))
    return call(body, pos, (1,), ins, outs, flops=10 * n * NX * cap * LANES * width)


def weight_specs(mats, other):
    half = (lambda pos: 1 - pos[3]) if other else (lambda pos: pos[3])
    specs = []
    for i, w in enumerate(mats):
        rows, cols = w.shape[1], w.shape[2]
        if i < 2:
            spec = pl.BlockSpec((1, rows, cols // 2), lambda e, pos: (e, 0, half(pos)))
        else:
            spec = pl.BlockSpec((1, rows // 2, cols), lambda e, pos: (e, half(pos), 0))
        specs.append((w, spec))
    return specs


def products_of(left, weights):
    half = left.shape[1] // 2
    tokens, cotangents = left[:, :half], left[:, half:]
    for i in range(3):
        yield i, dot(tokens if i < 2 else cotangents, weights[i][0], 1, 0 if i < 2 else 1)


def partial_other(pos, pieces, mats):
    _, part, width = pieces[0].shape
    rows = NX * part

    def body(pos_ref, *refs):
        ins, weights, (theirs, joined) = refs[:NX], refs[NX : NX + 3], refs[NX + 3 :]
        left = jnp.concatenate([r[0] for r in ins], axis=0)
        joined[0] = left
        for i, out in products_of(left, weights):
            for y in range(NY):
                theirs[y, i, 0] = out[:, y * LANES : (y + 1) * LANES].astype(BF16)

    ins = [(p, pl.BlockSpec((1, part, width), lambda e, pos: (e, 0, 0))) for p in pieces]
    outs = [
        (
            sds((NY, 3, 2, rows, LANES)),
            pl.BlockSpec((NY, 3, 1, rows, LANES), lambda e, pos: (0, 0, e, 0, 0)),
        ),
        (sds((2, rows, width)), pl.BlockSpec((1, rows, width), lambda e, pos: (e, 0, 0))),
    ]
    flops = 6 * rows * width * NY * LANES
    return call(body, pos, (2,), ins + weight_specs(mats, True), outs, flops=flops)


def partial_own(pos, joined, mats, got):
    _, rows, width = joined.shape

    def body(pos_ref, joined_ref, *refs):
        weights, got_ref, outs, hold = refs[:3], refs[3], refs[4:-1], refs[-1]
        for i, out in products_of(joined_ref[0], weights):
            for y in range(NY):
                hold[y] = out[:, y * LANES : (y + 1) * LANES]
            for k in range(NY):
                at = lax.rem(pos_ref[2] + k, NY)
                outs[k][i, 0] = (hold[at] + got_ref[at, i, 0].astype(F32)).astype(BF16)

    ins = [(joined, pl.BlockSpec((1, rows, width), lambda e, pos: (e, 0, 0)))]
    ins += weight_specs(mats, False)
    ins += [
        (got, pl.BlockSpec((NY, 3, 1, rows, LANES), lambda e, pos: (0, 0, e, 0, 0))),
    ]
    outs = [
        (sds((3, 2, rows, LANES)), pl.BlockSpec((3, 1, rows, LANES), lambda e, pos: (0, e, 0, 0)))
        for _ in range(NY)
    ]
    scratch = [pltpu.VMEM((NY, rows, LANES), F32)]
    return call(body, pos, (2,), ins, outs, scratch, flops=6 * rows * width * NY * LANES)


def units(pos, terms):
    rows = terms[0].shape[2]

    def body(pos_ref, *refs):
        def total(i):
            out = refs[0][i, 0].astype(F32)
            for r in refs[1:NY]:
                out = out + r[i, 0].astype(F32)
            return out

        gate, up, hid = total(0), total(1), total(2)
        s = 1.0 / (1.0 + jnp.exp(-gate))
        silu = gate * s
        refs[NY][0, 0] = (silu * up).astype(BF16)
        refs[NY][0, 1] = (hid * up * s * (1.0 + gate * (1.0 - s))).astype(BF16)
        refs[NY][0, 2] = (hid * silu).astype(BF16)

    spec = pl.BlockSpec((3, 1, rows, LANES), lambda e, pos: (0, e, 0, 0))
    out = pl.BlockSpec((1, 3, rows, LANES), lambda e, pos: (e, 0, 0, 0))
    return call(body, pos, (2,), [(t, spec) for t in terms], [(sds((2, 3, rows, LANES)), out)])[0]


def expert_rows(pos, mine, others, mats, part):
    rows = mine[0].shape[2]
    hidden = 2 * NY * LANES
    width = mats[2].shape[2]

    def body(pos_ref, *refs):
        ins, other, weights = refs[:NY], refs[NY], refs[NY + 1 : NY + 4]
        outs, fulls = refs[NY + 4 : NY + 4 + NX], refs[NY + 4 + NX :]
        y, c = pos_ref[2], pos_ref[3]
        for i in range(3):
            for k in range(NY):
                behind = lax.rem(y + NY - k, NY)
                at = pl.multiple_of((c * NY + behind) * LANES, LANES)
                fulls[i][0, :, pl.ds(at, LANES)] = ins[k][0, i]
                at = pl.multiple_of(((1 - c) * NY + behind) * LANES, LANES)
                fulls[i][0, :, pl.ds(at, LANES)] = other[k, 0, i]
        out = dot(fulls[0][0], weights[2][0], 1, 0).astype(BF16)
        back = dot(fulls[1][0], weights[0][0], 1, 1) + dot(fulls[2][0], weights[1][0], 1, 1)
        back = back.astype(BF16)
        for k in range(NX):
            outs[k][0, :, :width] = out[k * part : (k + 1) * part]
            outs[k][0, :, width:] = back[k * part : (k + 1) * part]

    ins = [(s, pl.BlockSpec((1, 3, rows, LANES), lambda e, pos: (e, 0, 0, 0))) for s in mine]
    ins += [
        (others, pl.BlockSpec((NY, 1, 3, rows, LANES), lambda e, pos: (0, e, 0, 0, 0))),
    ]
    ins += [(w, pl.BlockSpec((1,) + w.shape[1:], lambda e, pos: (e, 0, 0))) for w in mats]
    outs = [
        (
            sds((2, part, 2 * width)),
            pl.BlockSpec((1, part, 2 * width), lambda e, pos: (e, 0, 0)),
        )
        for _ in range(NX)
    ]
    outs += [
        (sds((2, rows, hidden)), pl.BlockSpec((1, rows, hidden), lambda e, pos: (e, 0, 0)))
        for _ in range(3)
    ]
    got = call(body, pos, (2,), ins, outs, flops=12 * rows * width * hidden)
    return got[:NX], got[NX:]


def weight_grad(pos, lefts, rights, side, left_wide):
    n = len(lefts)
    a, b = lefts[0].shape[2], rights[0].shape[2]
    ba, bb = (a // 2, b // 2)

    def body(pos_ref, *refs):
        total = dot(refs[0][0], refs[n][0], 0, 0)
        for i in range(1, n):
            total = total + dot(refs[i][0], refs[n + i][0], 0, 0)
        refs[2 * n][0] = total.astype(BF16)

    def spec(v, size, cut):
        return pl.BlockSpec((1, v.shape[1], size), lambda e, h, pos: (e, 0, h if cut else side))

    ins = [(v, spec(v, ba, left_wide)) for v in lefts]
    ins += [(v, spec(v, bb, not left_wide)) for v in rights]
    out = pl.BlockSpec(
        (1, ba, bb), lambda e, h, pos: (e, h if left_wide else 0, 0 if left_wide else h)
    )
    shape = (2, a, b // 2) if left_wide else (2, a // 2, b)
    rows = sum(v.shape[1] for v in lefts)
    return call(body, pos, (2, 2), ins, [(sds(shape), out)], flops=2 * rows * a * b)[0]


def spread(pieces, sign):
    return [pieces[0]] + [
        lax.ppermute(pieces[k], "expert", x_shift(sign * k)) for k in range(1, NX)
    ]


def per_device(
    tokens, expert_ids, combine_weight, gate_weight, up_weight, down_weight, out_cotangent
):
    tok_rows, width = tokens.shape
    top_count = expert_ids.shape[1]
    cap = 3 * tok_rows * top_count // (2 * gate_weight.shape[0] * NZ * NX)
    group, share = lax.axis_index("expert"), lax.axis_index("tensor")
    pos = jnp.stack([group // NX, group % NX, share // 2, share % 2]).astype(jnp.int32)
    mats = [gate_weight, up_weight, down_weight]

    ids = expert_ids.T
    weight = combine_weight.T
    high = lax.reduce_precision(weight, 8, 7)
    middle = lax.reduce_precision(weight - high, 8, 7)
    low = weight - high - middle
    meta = jnp.concatenate([ids.astype(F32), high, middle, low], axis=1).astype(BF16)
    meta = jnp.pad(meta, ((0, 16 - top_count), (0, 2 * width - 4 * tok_rows)))
    block = {0: jnp.concatenate([jnp.concatenate([tokens, out_cotangent], axis=1), meta], axis=0)}
    for j in range(1, NZ // 2 + 1):
        block[j] = lax.ppermute(block[j - 1], "expert", z_shift(1))
        if j < NZ // 2:
            block[NZ - j] = lax.ppermute(block[(NZ - j + 1) % NZ], "expert", z_shift(-1))

    sums = {}
    joined, acts, gates, ups = [], [], [], []
    for offsets in CHUNKS:
        blocks = [block[j] for j in offsets]
        pieces = spread(dispatch(pos, blocks, cap), 1)
        theirs, rows = partial_other(pos, pieces, mats)
        joined.append(rows)
        parts = partial_own(pos, rows, mats, lax.ppermute(theirs, "tensor", flip(1)))
        terms = [parts[0]] + [lax.ppermute(parts[k], "tensor", y_shift(k)) for k in (2, 1, 3)]
        own = units(pos, terms)
        mine = [own] + [lax.ppermute(own, "tensor", y_shift(k)) for k in range(1, NY)]
        others = lax.ppermute(jnp.stack(mine), "tensor", flip(1))
        pieces, fulls = expert_rows(pos, mine, others, mats, len(offsets) * cap)
        for kept, full in zip((acts, gates, ups), fulls):
            kept.append(full)
        for j, value in zip(offsets, combine(pos, blocks, spread(pieces, -1), offsets, cap)):
            sums[j] = value if j == 0 else lax.ppermute(value, "expert", z_shift(-j))

    both = sum(sums[j][:tok_rows].astype(F32) for j in range(NZ))
    mixed, token_grad = both[:, :width].astype(BF16), both[:, width:].astype(BF16)

    grads = jnp.zeros(ids.shape, F32)
    for j in range(NZ):
        table = sums[j][tok_rows : tok_rows + 8, :LANES].astype(F32)
        if j:
            table = table + sums[j][tok_rows + 8 :, :LANES].astype(F32)
        for k in range(NX):
            for e in range(2):
                expert = ((pos[0] + j) % NZ * NX + (pos[1] + k) % NX) * 2 + e
                grads = grads + jnp.where(ids == expert, table[k * 2 + e][None, :], 0.0)
    for mask in (1, 2, 4):
        grads = grads + lax.ppermute(grads, "tensor", flip(mask))

    gate_grad = weight_grad(pos, joined, gates, 0, False)
    up_grad = weight_grad(pos, joined, ups, 0, False)
    down_grad = weight_grad(pos, acts, joined, 1, True)
    return (mixed, token_grad, grads.T, gate_grad, up_grad, down_grad)


def solution(mesh):
    placed = (
        P("expert", "tensor"),
        P("expert", None),
        P("expert", None),
        P("expert", "tensor", None),
        P("expert", "tensor", None),
        P("expert", None, "tensor"),
        P("expert", "tensor"),
    )
    return jax.shard_map(
        per_device,
        mesh=mesh,
        in_specs=placed,
        out_specs=(
            P("expert", "tensor"),
            P("expert", "tensor"),
            P("expert", None),
            P("expert", "tensor", None),
            P("expert", "tensor", None),
            P("expert", None, "tensor"),
        ),
        check_vma=False,
    )
```

```python
import jax
import jax.numpy as jnp
from jax import lax
from jax.experimental import pallas as pl
from jax.experimental.pallas import tpu as pltpu
from jax.sharding import PartitionSpec as P

NZ, NX, NY = 8, 4, 4
CHUNKS = ((4, 3, 5, 6), (0, 1, 7, 2))
LANES = 128
F32, BF16 = jnp.float32, jnp.bfloat16


def z_shift(k):
    return [(z * NX + x, (z + k) % NZ * NX + x) for z in range(NZ) for x in range(NX)]


def x_groups():
    return [[z * NX + x for x in range(NX)] for z in range(NZ)]


def y_shift(k):
    return [(y * 2 + c, (y + k) % NY * 2 + c) for y in range(NY) for c in range(2)]


def flip(mask):
    return [(i, i ^ mask) for i in range(NY * 2)]


def call(body, pos, grid, ins, outs, scratch=(), flops=0, after=()):
    first, extra = len(ins), len(after)
    ins = list(ins) + [(a, pl.BlockSpec(memory_space=pl.ANY)) for a in after]
    arrays = [a for a, _ in ins]
    inner = body

    def body(pos_ref, *refs):
        inner(pos_ref, *refs[:first], *refs[first + extra :])

    moved = sum(a.size * a.dtype.itemsize for a in arrays[:first]) + sum(
        s.size * s.dtype.itemsize for s, _ in outs
    )
    return pl.pallas_call(
        body,
        out_shape=[s for s, _ in outs],
        grid_spec=pltpu.PrefetchScalarGridSpec(
            num_scalar_prefetch=1,
            grid=grid,
            in_specs=[s for _, s in ins],
            out_specs=[s for _, s in outs],
            scratch_shapes=list(scratch),
        ),
        compiler_params=pltpu.CompilerParams(vmem_limit_bytes=56 << 20),
        cost_estimate=pl.CostEstimate(flops=1, bytes_accessed=1, transcendentals=0),
    )(pos, *arrays)


def whole(shape):
    return pl.BlockSpec(shape, lambda i, pos: (0,) * len(shape))


def sds(shape, dtype=BF16):
    return jax.ShapeDtypeStruct(shape, dtype)


def dot(a, b, ca, cb):
    return lax.dot_general(a, b, (((ca,), (cb,)), ((), ())), preferred_element_type=F32)


def triangle():
    rows = lax.broadcasted_iota(jnp.int32, (LANES, LANES), 0)
    cols = lax.broadcasted_iota(jnp.int32, (LANES, LANES), 1)
    return jnp.where(rows < cols, 1.0, 0.0).astype(BF16)


def slots(meta, pos, cap):
    ids = meta[:8, :LANES]
    weight = meta[:8, LANES : 2 * LANES] + meta[:8, 2 * LANES : 3 * LANES] + meta[:8, 3 * LANES :]
    named, weights = [], []
    for k in range(NX):
        for e in range(2):
            expert = (pos[0] * NX + k) * 2 + e
            hit = ids == expert.astype(F32)
            named.append(jnp.sum(jnp.where(hit, 1.0, 0.0), axis=0, keepdims=True))
            weights.append(jnp.sum(jnp.where(hit, weight, 0.0), axis=0, keepdims=True))
    all_named = jnp.concatenate(named, axis=0)
    place = dot(all_named.astype(BF16), triangle(), 1, 0)
    place = jnp.where(all_named > 0.5, place, -1.0)
    count = lax.broadcasted_iota(jnp.int32, (cap, LANES), 0).astype(F32)
    tables = [jnp.where(count == place[q : q + 1], 1.0, 0.0) for q in range(2 * NX)]
    return tables, weights


def dispatch(pos, blocks, cap, after):
    n, width = len(blocks), blocks[0].shape[1]
    half = width // 2

    def body(pos_ref, *refs):
        p = (pos_ref[0], pos_ref[1])
        rows = []
        for i in range(n):
            meta = refs[i][LANES : LANES + 16, 0 : 4 * LANES].astype(F32)
            tables, weights = slots(meta, p, cap)
            table = jnp.concatenate(tables, axis=0)
            taken = dot(table.astype(BF16), refs[i][0:LANES, :], 1, 0)
            scale = jnp.concatenate(
                [jnp.sum(t * w, axis=1, keepdims=True) for t, w in zip(tables, weights)], axis=0
            )
            rows.append((taken[:, :half], taken[:, half:] * scale))
        for k in range(NX):
            for e in range(2):
                at = (k * 2 + e) * cap
                for side in range(2):
                    refs[n][k, e, :, side * half : (side + 1) * half] = jnp.concatenate(
                        [r[side][at : at + cap] for r in rows], axis=0
                    ).astype(BF16)

    ins = [(b, whole(b.shape)) for b in blocks]
    shape = (NX, 2, n * cap, width)
    outs = [(sds(shape), whole(shape))]
    flops = 4 * n * NX * cap * LANES * width
    return call(body, pos, (1,), ins, outs, flops=flops, after=after)[0]


def combine(pos, blocks, pieces, offsets, cap, after):
    n, width = len(blocks), pieces.shape[3]
    half = width // 2

    def body(pos_ref, *refs):
        p = (pos_ref[0], pos_ref[1])
        pieces_in, outs = refs[n], refs[n + 1 :]
        wide = [[pieces_in[k, e].astype(F32) for e in range(2)] for k in range(NX)]
        for i in range(n):
            meta = refs[i][LANES : LANES + 16, 0 : 4 * LANES].astype(F32)
            tables, weights = slots(meta, p, cap)
            table = jnp.concatenate(tables, axis=0).astype(BF16)
            rows = jnp.concatenate(
                [wide[k][e][i * cap : (i + 1) * cap] for k in range(NX) for e in range(2)], axis=0
            )
            rows16 = rows.astype(BF16)
            scaled = jnp.concatenate([t * w for t, w in zip(tables, weights)], axis=0)
            high = scaled.astype(BF16)
            low = (scaled - high.astype(F32)).astype(BF16)
            mixed = dot(high, rows16[:, :half], 0, 0) + dot(low, rows16[:, :half], 0, 0)
            back = dot(table, rows16[:, half:], 0, 0)
            picked = dot(table, refs[i][0:LANES, half:], 1, 0)
            each = jnp.sum(picked * rows[:, :half], axis=1, keepdims=True)
            grads = jnp.concatenate(
                [
                    jnp.sum(t * each[q * cap : (q + 1) * cap], axis=0, keepdims=True)
                    for q, t in enumerate(tables)
                ]
                + [jnp.zeros((8 - 2 * NX, LANES), F32)] * (2 * NX < 8),
                axis=0,
            )
            kind = F32 if offsets[i] == 0 else BF16
            outs[i][:, :half] = mixed.astype(kind)
            outs[i][:, half:] = back.astype(kind)
            outs[n + i][...] = grads

    ins = [(b, whole(b.shape)) for b in blocks]
    ins += [(pieces, whole(pieces.shape))]
    outs = [sds((LANES, width), F32 if j == 0 else BF16) for j in offsets]
    outs += [sds((8, LANES), F32) for _ in offsets]
    outs = [(o, whole(o.shape)) for o in outs]
    flops = 10 * n * NX * cap * LANES * width
    got = call(body, pos, (1,), ins, outs, flops=flops, after=after)
    return got[:n], got[n:]


def weight_specs(mats, other):
    half = (lambda pos: 1 - pos[3]) if other else (lambda pos: pos[3])
    specs = []
    for i, w in enumerate(mats):
        rows, cols = w.shape[1], w.shape[2]
        if i < 2:
            spec = pl.BlockSpec((1, rows, cols // 2), lambda e, pos: (e, 0, half(pos)))
        else:
            spec = pl.BlockSpec((1, rows // 2, cols), lambda e, pos: (e, half(pos), 0))
        specs.append((w, spec))
    return specs


def products_of(left, weights):
    half = left.shape[1] // 2
    tokens, cotangents = left[:, :half], left[:, half:]
    for i in range(3):
        yield i, dot(tokens if i < 2 else cotangents, weights[i][0], 1, 0 if i < 2 else 1)


def partial_other(pos, pieces, mats, after):
    _, _, part, width = pieces.shape
    rows = NX * part

    def body(pos_ref, *refs):
        rows_in, weights, (theirs, joined) = refs[0], refs[1:4], refs[4:]
        left = jnp.concatenate([rows_in[k, 0] for k in range(NX)], axis=0)
        joined[0] = left
        for i, out in products_of(left, weights):
            for y in range(NY):
                theirs[y, i, 0] = out[:, y * LANES : (y + 1) * LANES].astype(BF16)

    ins = [(pieces, pl.BlockSpec((NX, 1, part, width), lambda e, pos: (0, e, 0, 0)))]
    outs = [
        (
            sds((NY, 3, 2, rows, LANES)),
            pl.BlockSpec((NY, 3, 1, rows, LANES), lambda e, pos: (0, 0, e, 0, 0)),
        ),
        (sds((2, rows, width)), pl.BlockSpec((1, rows, width), lambda e, pos: (e, 0, 0))),
    ]
    flops = 6 * rows * width * NY * LANES
    return call(body, pos, (2,), ins + weight_specs(mats, True), outs, flops=flops, after=after)


def partial_own(pos, joined, mats, got):
    _, rows, width = joined.shape

    def body(pos_ref, joined_ref, *refs):
        weights, got_ref, outs, hold = refs[:3], refs[3], refs[4:-1], refs[-1]
        for i, out in products_of(joined_ref[0], weights):
            for y in range(NY):
                hold[y] = out[:, y * LANES : (y + 1) * LANES]
            for k in range(NY):
                at = lax.rem(pos_ref[2] + k, NY)
                outs[k][i, 0] = (hold[at] + got_ref[at, i, 0].astype(F32)).astype(BF16)

    ins = [(joined, pl.BlockSpec((1, rows, width), lambda e, pos: (e, 0, 0)))]
    ins += weight_specs(mats, False)
    ins += [
        (got, pl.BlockSpec((NY, 3, 1, rows, LANES), lambda e, pos: (0, 0, e, 0, 0))),
    ]
    outs = [
        (sds((3, 2, rows, LANES)), pl.BlockSpec((3, 1, rows, LANES), lambda e, pos: (0, e, 0, 0)))
        for _ in range(NY)
    ]
    scratch = [pltpu.VMEM((NY, rows, LANES), F32)]
    return call(body, pos, (2,), ins, outs, scratch, flops=6 * rows * width * NY * LANES)


def units(pos, terms, after):
    rows = terms[0].shape[2]

    def body(pos_ref, *refs):
        def total(i):
            out = refs[0][i, 0].astype(F32)
            for r in refs[1:NY]:
                out = out + r[i, 0].astype(F32)
            return out

        gate, up, hid = total(0), total(1), total(2)
        s = 1.0 / (1.0 + jnp.exp(-gate))
        silu = gate * s
        refs[NY][0, 0] = (silu * up).astype(BF16)
        refs[NY][0, 1] = (hid * up * s * (1.0 + gate * (1.0 - s))).astype(BF16)
        refs[NY][0, 2] = (hid * silu).astype(BF16)

    spec = pl.BlockSpec((3, 1, rows, LANES), lambda e, pos: (0, e, 0, 0))
    out = pl.BlockSpec((1, 3, rows, LANES), lambda e, pos: (e, 0, 0, 0))
    outs = [(sds((2, 3, rows, LANES)), out)]
    return call(body, pos, (2,), [(t, spec) for t in terms], outs, after=after)[0]


def expert_rows(pos, mine, others, mats, part, after):
    rows = mine[0].shape[2]
    hidden = 2 * NY * LANES
    width = mats[2].shape[2]

    def body(pos_ref, *refs):
        ins, other, weights = refs[:NY], refs[NY], refs[NY + 1 : NY + 4]
        outs, fulls = refs[NY + 4], refs[NY + 5 :]
        y, c = pos_ref[2], pos_ref[3]
        for i in range(3):
            for k in range(NY):
                behind = lax.rem(y + NY - k, NY)
                at = pl.multiple_of((c * NY + behind) * LANES, LANES)
                fulls[i][0, :, pl.ds(at, LANES)] = ins[k][0, i]
                at = pl.multiple_of(((1 - c) * NY + behind) * LANES, LANES)
                fulls[i][0, :, pl.ds(at, LANES)] = other[k, 0, i]
        out = dot(fulls[0][0], weights[2][0], 1, 0).astype(BF16)
        back = dot(fulls[1][0], weights[0][0], 1, 1) + dot(fulls[2][0], weights[1][0], 1, 1)
        back = back.astype(BF16)
        for k in range(NX):
            outs[k, 0, :, :width] = out[k * part : (k + 1) * part]
            outs[k, 0, :, width:] = back[k * part : (k + 1) * part]

    ins = [(s, pl.BlockSpec((1, 3, rows, LANES), lambda e, pos: (e, 0, 0, 0))) for s in mine]
    ins += [
        (others, pl.BlockSpec((NY, 1, 3, rows, LANES), lambda e, pos: (0, e, 0, 0, 0))),
    ]
    ins += [(w, pl.BlockSpec((1,) + w.shape[1:], lambda e, pos: (e, 0, 0))) for w in mats]
    outs = [
        (
            sds((NX, 2, part, 2 * width)),
            pl.BlockSpec((NX, 1, part, 2 * width), lambda e, pos: (0, e, 0, 0)),
        )
    ]
    outs += [
        (sds((2, rows, hidden)), pl.BlockSpec((1, rows, hidden), lambda e, pos: (e, 0, 0)))
        for _ in range(3)
    ]
    got = call(body, pos, (2,), ins, outs, flops=12 * rows * width * hidden, after=after)
    return got[0], got[1:]


def weight_grad(pos, lefts, rights, side, left_wide):
    n = len(lefts)
    a, b = lefts[0].shape[2], rights[0].shape[2]
    ba, bb = (a // 2, b // 2)

    def body(pos_ref, *refs):
        total = dot(refs[0][0], refs[n][0], 0, 0)
        for i in range(1, n):
            total = total + dot(refs[i][0], refs[n + i][0], 0, 0)
        refs[2 * n][0] = total.astype(BF16)

    def spec(v, size, cut):
        return pl.BlockSpec((1, v.shape[1], size), lambda e, h, pos: (e, 0, h if cut else side))

    ins = [(v, spec(v, ba, left_wide)) for v in lefts]
    ins += [(v, spec(v, bb, not left_wide)) for v in rights]
    out = pl.BlockSpec(
        (1, ba, bb), lambda e, h, pos: (e, h if left_wide else 0, 0 if left_wide else h)
    )
    shape = (2, a, b // 2) if left_wide else (2, a // 2, b)
    rows = sum(v.shape[1] for v in lefts)
    return call(body, pos, (2, 2), ins, [(sds(shape), out)], flops=2 * rows * a * b)[0]


def exchanged(pieces):
    return lax.all_to_all(pieces, "expert", 0, 0, axis_index_groups=x_groups(), tiled=True)


def scattered(parts):
    return [parts[0]] + [lax.ppermute(parts[k], "tensor", y_shift(k)) for k in range(1, NY)]


def gathered(own):
    return [own] + [lax.ppermute(own, "tensor", y_shift(k)) for k in range(1, NY)]


def per_device(
    tokens, expert_ids, combine_weight, gate_weight, up_weight, down_weight, out_cotangent
):
    tok_rows, width = tokens.shape
    top_count = expert_ids.shape[1]
    cap = 3 * tok_rows * top_count // (2 * gate_weight.shape[0] * NZ * NX)
    group, share = lax.axis_index("expert"), lax.axis_index("tensor")
    pos = jnp.stack([group // NX, group % NX, share // 2, share % 2]).astype(jnp.int32)
    mats = [gate_weight, up_weight, down_weight]

    ids = expert_ids.T
    weight = combine_weight.T
    high = lax.reduce_precision(weight, 8, 7)
    middle = lax.reduce_precision(weight - high, 8, 7)
    low = weight - high - middle
    meta = jnp.concatenate([ids.astype(F32), high, middle, low], axis=1).astype(BF16)
    meta = jnp.pad(meta, ((0, 16 - top_count), (0, 2 * width - 4 * tok_rows)))
    block = {0: jnp.concatenate([jnp.concatenate([tokens, out_cotangent], axis=1), meta], axis=0)}
    for j in range(1, NZ // 2 + 1):
        block[j] = lax.ppermute(block[j - 1], "expert", z_shift(1))
        if j < NZ // 2:
            block[NZ - j] = lax.ppermute(block[(NZ - j + 1) % NZ], "expert", z_shift(-1))

    part = NZ // 2 * cap
    near, far = [block[j] for j in CHUNKS[1]], [block[j] for j in CHUNKS[0]]

    def returned(offsets, values):
        return {j: v if j == 0 else lax.ppermute(v, "expert", z_shift(-j)) for j, v in zip(offsets, values)}

    rows_b = dispatch(pos, near, cap, [])
    rows_a = dispatch(pos, far, cap, [rows_b])
    theirs_a, joined_a = partial_other(pos, exchanged(rows_a), mats, [])
    parts_a = partial_own(pos, joined_a, mats, lax.ppermute(theirs_a, "tensor", flip(1)))
    terms_a = scattered(parts_a)
    theirs_b, joined_b = partial_other(pos, exchanged(rows_b), mats, terms_a[1::2])
    parts_b = partial_own(pos, joined_b, mats, lax.ppermute(theirs_b, "tensor", flip(1)))
    terms_b = scattered(parts_b)
    mine_a = gathered(units(pos, terms_a, terms_b[1::2]))
    mine_b = gathered(units(pos, terms_b, mine_a[1::2]))
    stack_a, _ = lax.optimization_barrier((jnp.stack(mine_a), mine_b[0]))
    others_a = lax.ppermute(stack_a, "tensor", flip(1))
    out_a, full_a = expert_rows(pos, mine_a, others_a, mats, part, [])
    sums_a, dots_a = combine(pos, far, exchanged(out_a), CHUNKS[0], cap, [])
    others_b = lax.ppermute(jnp.stack(mine_b), "tensor", flip(1))
    out_b, full_b = expert_rows(pos, mine_b, others_b, mats, part, [sums_a[0]])
    sums = returned(CHUNKS[0], sums_a)
    dots = returned(CHUNKS[0], dots_a)
    back_b = exchanged(out_b)
    sums_b, dots_b = combine(pos, near, back_b, CHUNKS[1], cap, list(sums.values()))
    dots |= returned(CHUNKS[1], dots_b)
    sums |= returned(CHUNKS[1], sums_b)

    grads = jnp.zeros(ids.shape, F32)
    for j in range(NZ):
        for k in range(NX):
            for e in range(2):
                expert = ((pos[0] + j) % NZ * NX + k) * 2 + e
                grads = grads + jnp.where(ids == expert, dots[j][k * 2 + e][None, :], 0.0)
    joined = [joined_a, joined_b]
    acts, gates, ups = zip(full_a, full_b)
    gate_grad = weight_grad(pos, joined, gates, 0, False)
    up_grad = weight_grad(pos, joined, ups, 0, False)
    grads, _ = lax.optimization_barrier((grads, (sums[1], sums[NZ - 1], up_grad)))
    grads = grads + lax.ppermute(grads, "tensor", flip(1))
    far1, far2, far3 = [lax.ppermute(grads, "tensor", flip(m)) for m in (2, 4, 6)]
    grads = (grads + far1) + (far2 + far3)
    down_grad = weight_grad(pos, acts, joined, 1, True)

    both = sum(sums[j].astype(F32) for j in range(NZ))
    mixed, token_grad = both[:, :width].astype(BF16), both[:, width:].astype(BF16)

    return (mixed, token_grad, grads.T, gate_grad, up_grad, down_grad)


def solution(mesh):
    placed = (
        P("expert", "tensor"),
        P("expert", None),
        P("expert", None),
        P("expert", "tensor", None),
        P("expert", "tensor", None),
        P("expert", None, "tensor"),
        P("expert", "tensor"),
    )
    return jax.shard_map(
        per_device,
        mesh=mesh,
        in_specs=placed,
        out_specs=(
            P("expert", "tensor"),
            P("expert", "tensor"),
            P("expert", None),
            P("expert", "tensor", None),
            P("expert", "tensor", None),
            P("expert", None, "tensor"),
        ),
        check_vma=False,
    )
```

```python
import jax
import jax.numpy as jnp
from jax import lax
from jax.experimental import pallas as pl
from jax.experimental.pallas import tpu as pltpu
from jax.sharding import PartitionSpec as P

NZ, NX, NY = 8, 4, 4
LANES = 128
F32, BF16 = jnp.float32, jnp.bfloat16


def z_shift(k):
    return [(z * NX + x, (z + k) % NZ * NX + x) for z in range(NZ) for x in range(NX)]


def x_groups():
    return [[z * NX + x for x in range(NX)] for z in range(NZ)]


def y_shift(k):
    return [(y * 2 + c, (y + k) % NY * 2 + c) for y in range(NY) for c in range(2)]


def flip(mask):
    return [(i, i ^ mask) for i in range(NY * 2)]


def call(body, pos, grid, ins, outs, scratch=(), flops=0, after=()):
    first, extra = len(ins), len(after)
    ins = list(ins) + [(a, pl.BlockSpec(memory_space=pl.ANY)) for a in after]
    arrays = [a for a, _ in ins]
    inner = body

    def body(pos_ref, *refs):
        inner(pos_ref, *refs[:first], *refs[first + extra :])

    moved = sum(a.size * a.dtype.itemsize for a in arrays[:first]) + sum(
        s.size * s.dtype.itemsize for s, _ in outs
    )
    return pl.pallas_call(
        body,
        out_shape=[s for s, _ in outs],
        grid_spec=pltpu.PrefetchScalarGridSpec(
            num_scalar_prefetch=1,
            grid=grid,
            in_specs=[s for _, s in ins],
            out_specs=[s for _, s in outs],
            scratch_shapes=list(scratch),
        ),
        compiler_params=pltpu.CompilerParams(vmem_limit_bytes=56 << 20),
        cost_estimate=pl.CostEstimate(flops=1, bytes_accessed=1, transcendentals=0),
    )(pos, *arrays)


def whole(shape):
    return pl.BlockSpec(shape, lambda i, pos: (0,) * len(shape))


def sds(shape, dtype=BF16):
    return jax.ShapeDtypeStruct(shape, dtype)


def dot(a, b, ca, cb):
    return lax.dot_general(a, b, (((ca,), (cb,)), ((), ())), preferred_element_type=F32)


def triangle():
    rows = lax.broadcasted_iota(jnp.int32, (LANES, LANES), 0)
    cols = lax.broadcasted_iota(jnp.int32, (LANES, LANES), 1)
    return jnp.where(rows < cols, 1.0, 0.0).astype(BF16)


def slots(meta, pos, cap):
    ids = meta[:8, :LANES]
    weight = meta[:8, LANES : 2 * LANES] + meta[:8, 2 * LANES : 3 * LANES] + meta[:8, 3 * LANES :]
    named, weights = [], []
    for k in range(NX):
        for e in range(2):
            expert = (pos[0] * NX + k) * 2 + e
            hit = ids == expert.astype(F32)
            named.append(jnp.sum(jnp.where(hit, 1.0, 0.0), axis=0, keepdims=True))
            weights.append(jnp.sum(jnp.where(hit, weight, 0.0), axis=0, keepdims=True))
    all_named = jnp.concatenate(named, axis=0)
    place = dot(all_named.astype(BF16), triangle(), 1, 0)
    place = jnp.where(all_named > 0.5, place, -1.0)
    count = lax.broadcasted_iota(jnp.int32, (cap, LANES), 0).astype(F32)
    tables = [jnp.where(count == place[q : q + 1], 1.0, 0.0) for q in range(2 * NX)]
    return tables, weights


def meta_spec():
    return pl.BlockSpec((16, 4 * LANES), lambda i, pos: (LANES // 16, 0))


def dispatch(pos, metas, blocks, cap, weighted, after=()):
    n, width = len(metas), blocks[0].shape[1]

    def body(pos_ref, *refs):
        p = (pos_ref[0], pos_ref[1])
        rows = []
        for i in range(n):
            tables, weights = slots(refs[i][...].astype(F32), p, cap)
            table = jnp.concatenate(tables, axis=0)
            taken = dot(table.astype(BF16), refs[n + i][0:LANES, :], 1, 0)
            if weighted:
                scale = jnp.concatenate(
                    [jnp.sum(t * w, axis=1, keepdims=True) for t, w in zip(tables, weights)], axis=0
                )
                taken = taken * scale
            rows.append(taken)
        for k in range(NX):
            for e in range(2):
                at = (k * 2 + e) * cap
                refs[2 * n][k, e] = jnp.concatenate(
                    [r[at : at + cap] for r in rows], axis=0
                ).astype(BF16)

    ins = [(m, meta_spec()) for m in metas] + [(b, whole(b.shape)) for b in blocks]
    outs = [(sds((NX, 2, n * cap, width)), whole((NX, 2, n * cap, width)))]
    return call(body, pos, (1,), ins, outs, after=after)[0]


def combine(pos, metas, pieces, cots, cap, after=()):
    n, width = len(metas), pieces.shape[3]
    mixing = cots is not None

    def body(pos_ref, *refs):
        p = (pos_ref[0], pos_ref[1])
        pieces_in = refs[n]
        cots_in = refs[n + 1 : n + 1 + n] if mixing else ()
        outs = refs[len(refs) - n :]
        wide = [[pieces_in[k, e].astype(F32) for e in range(2)] for k in range(NX)]
        for i in range(n):
            tables, weights = slots(refs[i][...].astype(F32), p, cap)
            table = jnp.concatenate(tables, axis=0)
            rows = jnp.concatenate(
                [wide[k][e][i * cap : (i + 1) * cap] for k in range(NX) for e in range(2)], axis=0
            )
            rows16 = rows.astype(BF16)
            if mixing:
                scaled = jnp.concatenate([t * w for t, w in zip(tables, weights)], axis=0)
                high = scaled.astype(BF16)
                low = (scaled - high.astype(F32)).astype(BF16)
                total = dot(high, rows16, 0, 0) + dot(low, rows16, 0, 0)
                picked = dot(table.astype(BF16), cots_in[i][...], 1, 0)
                each = jnp.sum(picked * rows, axis=1, keepdims=True)
                grads = jnp.concatenate(
                    [
                        jnp.sum(t * each[q * cap : (q + 1) * cap], axis=0, keepdims=True)
                        for q, t in enumerate(tables)
                    ]
                    + [jnp.zeros((8 - 2 * NX, LANES), F32)] * (2 * NX < 8),
                    axis=0,
                )
            else:
                total = dot(table.astype(BF16), rows16, 0, 0)
            if i == 0:
                outs[i][0:LANES, :] = total
                if mixing:
                    outs[i][LANES : LANES + 8, 0:LANES] = grads
            else:
                outs[i][0:LANES, :] = total.astype(BF16)
                if mixing:
                    top = grads.astype(BF16)
                    outs[i][LANES : LANES + 16, :] = jnp.zeros((16, width), BF16)
                    outs[i][LANES : LANES + 16, 0:LANES] = jnp.concatenate(
                        [top.astype(F32), grads - top.astype(F32)], axis=0
                    ).astype(BF16)

    ins = [(m, meta_spec()) for m in metas] + [(pieces, whole(pieces.shape))]
    if mixing:
        ins += [(b, whole(b.shape)) for b in cots]
    outs = [sds((LANES + 8 * mixing, width), F32)]
    outs += [sds((LANES + 16 * mixing, width))] * (n - 1)
    outs = [(o, whole(o.shape)) for o in outs]
    return call(body, pos, (1,), ins, outs, after=after)


def weight_spec(w, across, other):
    rows, cols = w.shape[1], w.shape[2]
    half = (lambda pos: 1 - pos[3]) if other else (lambda pos: pos[3])
    if across:
        return pl.BlockSpec((1, rows // 2, cols), lambda e, pos: (e, half(pos), 0))
    return pl.BlockSpec((1, rows, cols // 2), lambda e, pos: (e, 0, half(pos)))


def partial_other(pos, pieces, mats, across, after):
    m, (_, _, part, width) = len(mats), pieces.shape
    rows = NX * part

    def body(pos_ref, *refs):
        rows_in, weights, (theirs, joined) = refs[0], refs[1 : 1 + m], refs[1 + m :]
        left = jnp.concatenate([rows_in[k, 0] for k in range(NX)], axis=0)
        joined[0] = left
        for i in range(m):
            out = dot(left, weights[i][0], 1, 1 if across else 0).astype(BF16)
            for y in range(NY):
                theirs[y, i, 0] = out[:, y * LANES : (y + 1) * LANES]

    ins = [(pieces, pl.BlockSpec((NX, 1, part, width), lambda e, pos: (0, e, 0, 0)))]
    ins += [(w, weight_spec(w, across, True)) for w in mats]
    outs = [
        (
            sds((NY, m, 2, rows, LANES)),
            pl.BlockSpec((NY, m, 1, rows, LANES), lambda e, pos: (0, 0, e, 0, 0)),
        ),
        (sds((2, rows, width)), pl.BlockSpec((1, rows, width), lambda e, pos: (e, 0, 0))),
    ]
    return call(body, pos, (2,), ins, outs, after=after)


def partial_own(pos, joined, mats, got, across, after):
    m, (_, rows, width) = len(mats), joined.shape

    def body(pos_ref, joined_ref, *refs):
        weights, got_ref, outs, hold = refs[:m], refs[m], refs[m + 1 : -1], refs[-1]
        for i in range(m):
            out = dot(joined_ref[0], weights[i][0], 1, 1 if across else 0)
            for y in range(NY):
                hold[y, i] = out[:, y * LANES : (y + 1) * LANES]
        for k in range(NY):
            at = lax.rem(pos_ref[2] + k, NY)
            for i in range(m):
                outs[k][i, 0] = (hold[at, i] + got_ref[at, i, 0].astype(F32)).astype(BF16)

    ins = [(joined, pl.BlockSpec((1, rows, width), lambda e, pos: (e, 0, 0)))]
    ins += [(w, weight_spec(w, across, False)) for w in mats]
    ins += [
        (got, pl.BlockSpec((NY, m, 1, rows, LANES), lambda e, pos: (0, 0, e, 0, 0))),
    ]
    outs = [
        (sds((m, 2, rows, LANES)), pl.BlockSpec((m, 1, rows, LANES), lambda e, pos: (0, e, 0, 0)))
        for _ in range(NY)
    ]
    scratch = [pltpu.VMEM((NY, m, rows, LANES), F32)]
    return call(body, pos, (2,), ins, outs, scratch, after=after)


def scattered(parts):
    return [parts[0]] + [lax.ppermute(parts[k], "tensor", y_shift(k)) for k in range(1, NY)]


def term_sum(refs, i):
    total = refs[0][i, 0].astype(F32)
    for r in refs[1:]:
        total = total + r[i, 0].astype(F32)
    return total


def sigmoid(v):
    return 1.0 / (1.0 + jnp.exp(-v))


def term_specs(terms):
    m, _, rows, _ = terms[0].shape
    spec = pl.BlockSpec((m, 1, rows, LANES), lambda e, pos: (0, e, 0, 0))
    return [(t, spec) for t in terms]


def activated(pos, terms, after):
    rows = terms[0].shape[2]

    def body(pos_ref, *refs):
        gate, up = term_sum(refs[:NY], 0), term_sum(refs[:NY], 1)
        refs[NY][0, 0] = (gate * sigmoid(gate) * up).astype(BF16)

    outs = [
        (
            sds((2, 1, rows, LANES)),
            pl.BlockSpec((1, 1, rows, LANES), lambda e, pos: (e, 0, 0, 0)),
        )
    ]
    return call(body, pos, (2,), term_specs(terms), outs, after=after)[0]


def differed(pos, terms, hid_terms, after):
    rows = terms[0].shape[2]

    def body(pos_ref, *refs):
        gate, up = term_sum(refs[:NY], 0), term_sum(refs[:NY], 1)
        hid = term_sum(refs[NY : 2 * NY], 0)
        s = sigmoid(gate)
        refs[2 * NY][0, 0] = (hid * up * s * (1.0 + gate * (1.0 - s))).astype(BF16)
        refs[2 * NY][0, 1] = (hid * (gate * s)).astype(BF16)

    outs = [
        (
            sds((2, 2, rows, LANES)),
            pl.BlockSpec((1, 2, rows, LANES), lambda e, pos: (e, 0, 0, 0)),
        )
    ]
    ins = term_specs(terms) + term_specs(hid_terms)
    return call(body, pos, (2,), ins, outs, after=after)[0]


def gathered(own):
    return [own] + [lax.ppermute(own, "tensor", y_shift(k)) for k in range(1, NY)]


def products(pos, mine, others, mats, across, part, after):
    rows = mine[0].shape[2]
    m, hidden = len(mats), 2 * NY * LANES
    width = mats[0].shape[1] if across else mats[0].shape[2]

    def body(pos_ref, *refs):
        ins, other, weights = refs[:NY], refs[NY], refs[NY + 1 : NY + 1 + m]
        outs, fulls = refs[NY + 1 + m], refs[NY + 2 + m :]
        y, c = pos_ref[2], pos_ref[3]
        total = None
        for i in range(m):
            for k in range(NY):
                behind = lax.rem(y + NY - k, NY)
                at = pl.multiple_of((c * NY + behind) * LANES, LANES)
                fulls[i][0, :, pl.ds(at, LANES)] = ins[k][0, i]
                at = pl.multiple_of(((1 - c) * NY + behind) * LANES, LANES)
                fulls[i][0, :, pl.ds(at, LANES)] = other[k, 0, i]
            term = dot(fulls[i][0], weights[i][0], 1, 1 if across else 0)
            total = term if total is None else total + term
        total = total.astype(BF16)
        for k in range(NX):
            outs[k, 0] = total[k * part : (k + 1) * part]

    ins = [(s, pl.BlockSpec((1, m, rows, LANES), lambda e, pos: (e, 0, 0, 0))) for s in mine]
    ins += [(others, pl.BlockSpec((NY, 1, m, rows, LANES), lambda e, pos: (0, e, 0, 0, 0)))]
    ins += [(w, pl.BlockSpec((1,) + w.shape[1:], lambda e, pos: (e, 0, 0))) for w in mats]
    outs = [
        (
            sds((NX, 2, part, width)),
            pl.BlockSpec((NX, 1, part, width), lambda e, pos: (0, e, 0, 0)),
        )
    ]
    outs += [
        (sds((2, rows, hidden)), pl.BlockSpec((1, rows, hidden), lambda e, pos: (e, 0, 0)))
        for _ in range(m)
    ]
    got = call(body, pos, (2,), ins, outs, after=after)
    return got[0], got[1:]


def weight_grad(pos, left, right, left_wide, after):
    rows, a, b = left.shape[1], left.shape[2], right.shape[2]
    ba, bb = (a // 2, b) if left_wide else (a, b // 2)

    def body(pos_ref, left_ref, right_ref, out):
        out[0] = dot(left_ref[0], right_ref[0], 0, 0).astype(BF16)

    def spec(size, cut):
        return pl.BlockSpec((1, rows, size), lambda e, h, pos: (e, 0, h if cut else 0))

    ins = [(left, spec(ba, left_wide)), (right, spec(bb, not left_wide))]
    out = pl.BlockSpec(
        (1, ba, bb), lambda e, h, pos: (e, h if left_wide else 0, 0 if left_wide else h)
    )
    return call(body, pos, (2, 2), ins, [(sds((2, a, b)), out)], after=after)[0]


def exchanged(pieces):
    return lax.all_to_all(pieces, "expert", 0, 0, axis_index_groups=x_groups(), tiled=True)


def ring(own):
    block = {0: own}
    for j in range(1, NZ // 2 + 1):
        block[j] = lax.ppermute(block[j - 1], "expert", z_shift(1))
        if j < NZ // 2:
            block[NZ - j] = lax.ppermute(block[(NZ - j + 1) % NZ], "expert", z_shift(-1))
    return [block[j] for j in range(NZ)]


def returned(values):
    return [values[0]] + [lax.ppermute(values[j], "expert", z_shift(-j)) for j in range(1, NZ)]


def order(value, *after):
    return lax.optimization_barrier((value, after))[0]


def per_device(
    tokens, expert_ids, combine_weight, gate_weight, up_weight, down_weight, out_cotangent
):
    tok_rows, width = tokens.shape
    top_count = expert_ids.shape[1]
    cap = 3 * tok_rows * top_count // (2 * gate_weight.shape[0] * NZ * NX)
    group, share = lax.axis_index("expert"), lax.axis_index("tensor")
    pos = jnp.stack([group // NX, group % NX, share // 2, share % 2]).astype(jnp.int32)

    ids = expert_ids.T
    weight = combine_weight.T
    high = lax.reduce_precision(weight, 8, 7)
    middle = lax.reduce_precision(weight - high, 8, 7)
    low = weight - high - middle
    meta = jnp.concatenate([ids.astype(F32), high, middle, low], axis=1).astype(BF16)
    meta = jnp.pad(meta, ((0, 16 - top_count), (0, width - 4 * tok_rows)))
    part = NZ * cap

    toks = ring(jnp.concatenate([tokens, meta], axis=0))
    cots = ring(out_cotangent)
    far = NZ // 2
    rows = exchanged(dispatch(pos, toks, toks, cap, False, [cots[far], cots[far + 1]]))
    theirs, routed = partial_other(pos, rows, [gate_weight, up_weight], False, [])
    sent = dispatch(pos, toks, cots, cap, True, [theirs])
    parts = partial_own(
        pos, routed, [gate_weight, up_weight], lax.ppermute(theirs, "tensor", flip(1)), False, [sent]
    )
    terms = scattered(parts)
    theirs, cotangents = partial_other(pos, exchanged(sent), [down_weight], True, terms[1::2])
    parts = partial_own(
        pos, cotangents, [down_weight], lax.ppermute(theirs, "tensor", flip(1)), True, []
    )
    hid_terms = scattered(parts)
    act = activated(pos, terms, [parts[0]])
    diff = differed(pos, terms, hid_terms, [act])
    acts = gathered(order(act, diff))
    diffs = gathered(order(diff, *acts[1:]))
    others = lax.ppermute(jnp.stack(acts), "tensor", flip(1))
    out, (act_full,) = products(pos, acts, others, [down_weight], False, part, [diffs[0]])
    back = exchanged(out)
    others = lax.ppermute(jnp.stack(order(diffs, back)), "tensor", flip(1))
    sums = combine(pos, toks, back, cots, cap)
    mixed_parts = returned(sums)
    out, (gate_full, up_full) = products(
        pos, diffs, others, [gate_weight, up_weight], True, part, [sums[0]]
    )
    back = exchanged(out)
    late = order(mixed_parts, back)
    down_grad = weight_grad(pos, act_full, cotangents, True, [out])
    gate_grad = weight_grad(pos, routed, gate_full, False, [])
    up_grad = weight_grad(pos, routed, up_full, False, [])

    grads = jnp.zeros(ids.shape, F32)
    for j in range(NZ):
        table = late[j][tok_rows : tok_rows + 8, :LANES].astype(F32)
        if j:
            table = table + late[j][tok_rows + 8 :, :LANES].astype(F32)
        for k in range(NX):
            for e in range(2):
                expert = ((pos[0] + j) % NZ * NX + k) * 2 + e
                grads = grads + jnp.where(ids == expert, table[k * 2 + e][None, :], 0.0)

    done = [down_grad, gate_grad, up_grad]
    grad_parts = returned(combine(pos, toks, back, None, cap, done))
    grads = order(grads, grad_parts[NZ - 1], grad_parts[NZ - 2])
    grads = grads + lax.ppermute(grads, "tensor", flip(1))
    far1, far2, far3 = [lax.ppermute(grads, "tensor", flip(m)) for m in (2, 4, 6)]
    grads = (grads + far1) + (far2 + far3)
    mixed = sum(v[:tok_rows].astype(F32) for v in late).astype(BF16)
    token_grad = sum(v.astype(F32) for v in grad_parts).astype(BF16)
    return (mixed, token_grad, grads.T, gate_grad, up_grad, down_grad)


def solution(mesh):
    placed = (
        P("expert", "tensor"),
        P("expert", None),
        P("expert", None),
        P("expert", "tensor", None),
        P("expert", "tensor", None),
        P("expert", None, "tensor"),
        P("expert", "tensor"),
    )
    return jax.shard_map(
        per_device,
        mesh=mesh,
        in_specs=placed,
        out_specs=(
            P("expert", "tensor"),
            P("expert", "tensor"),
            P("expert", None),
            P("expert", "tensor", None),
            P("expert", "tensor", None),
            P("expert", None, "tensor"),
        ),
        check_vma=False,
    )
```

```python
import jax
import jax.numpy as jnp
from jax import lax
from jax.experimental import pallas as pl
from jax.experimental.pallas import tpu as pltpu
from jax.sharding import PartitionSpec as P

NZ, NX, NY = 8, 4, 4
LANES = 128
F32, BF16 = jnp.float32, jnp.bfloat16


def z_shift(k):
    return [(z * NX + x, (z + k) % NZ * NX + x) for z in range(NZ) for x in range(NX)]


def x_groups():
    return [[z * NX + x for x in range(NX)] for z in range(NZ)]


def y_shift(k):
    return [(y * 2 + c, (y + k) % NY * 2 + c) for y in range(NY) for c in range(2)]


def flip(mask):
    return [(i, i ^ mask) for i in range(NY * 2)]


def call(body, pos, grid, ins, outs, scratch=(), flops=0, after=()):
    first, extra = len(ins), len(after)
    ins = list(ins) + [(a, pl.BlockSpec(memory_space=pl.ANY)) for a in after]
    arrays = [a for a, _ in ins]
    inner = body

    def body(pos_ref, *refs):
        inner(pos_ref, *refs[:first], *refs[first + extra :])

    moved = sum(a.size * a.dtype.itemsize for a in arrays[:first]) + sum(
        s.size * s.dtype.itemsize for s, _ in outs
    )
    return pl.pallas_call(
        body,
        out_shape=[s for s, _ in outs],
        grid_spec=pltpu.PrefetchScalarGridSpec(
            num_scalar_prefetch=1,
            grid=grid,
            in_specs=[s for _, s in ins],
            out_specs=[s for _, s in outs],
            scratch_shapes=list(scratch),
        ),
        compiler_params=pltpu.CompilerParams(vmem_limit_bytes=56 << 20),
        cost_estimate=pl.CostEstimate(flops=1, bytes_accessed=1, transcendentals=0),
    )(pos, *arrays)


def whole(shape):
    return pl.BlockSpec(shape, lambda i, pos: (0,) * len(shape))


def sds(shape, dtype=BF16):
    return jax.ShapeDtypeStruct(shape, dtype)


def dot(a, b, ca, cb):
    return lax.dot_general(a, b, (((ca,), (cb,)), ((), ())), preferred_element_type=F32)


def triangle():
    rows = lax.broadcasted_iota(jnp.int32, (LANES, LANES), 0)
    cols = lax.broadcasted_iota(jnp.int32, (LANES, LANES), 1)
    return jnp.where(rows < cols, 1.0, 0.0).astype(BF16)


def slots(meta, pos, cap):
    ids = meta[:8, :LANES]
    weight = meta[:8, LANES : 2 * LANES] + meta[:8, 2 * LANES : 3 * LANES] + meta[:8, 3 * LANES :]
    named, weights = [], []
    for k in range(NX):
        for e in range(2):
            expert = (pos[0] * NX + k) * 2 + e
            hit = ids == expert.astype(F32)
            named.append(jnp.sum(jnp.where(hit, 1.0, 0.0), axis=0, keepdims=True))
            weights.append(jnp.sum(jnp.where(hit, weight, 0.0), axis=0, keepdims=True))
    all_named = jnp.concatenate(named, axis=0)
    place = dot(all_named.astype(BF16), triangle(), 1, 0)
    place = jnp.where(all_named > 0.5, place, -1.0)
    count = lax.broadcasted_iota(jnp.int32, (cap, LANES), 0).astype(F32)
    tables = [jnp.where(count == place[q : q + 1], 1.0, 0.0) for q in range(2 * NX)]
    return tables, weights


def meta_spec():
    return pl.BlockSpec((16, 4 * LANES), lambda i, pos: (LANES // 16, 0))


def dispatch(pos, metas, blocks, cap, weighted, after=()):
    n, width = len(metas), blocks[0].shape[1]

    def body(pos_ref, *refs):
        p = (pos_ref[0], pos_ref[1])
        rows = []
        for i in range(n):
            tables, weights = slots(refs[i][...].astype(F32), p, cap)
            table = jnp.concatenate(tables, axis=0)
            taken = dot(table.astype(BF16), refs[n + i][0:LANES, :], 1, 0)
            if weighted:
                scale = jnp.concatenate(
                    [jnp.sum(t * w, axis=1, keepdims=True) for t, w in zip(tables, weights)], axis=0
                )
                taken = taken * scale
            rows.append(taken)
        for k in range(NX):
            for e in range(2):
                at = (k * 2 + e) * cap
                refs[2 * n][k, e] = jnp.concatenate(
                    [r[at : at + cap] for r in rows], axis=0
                ).astype(BF16)

    ins = [(m, meta_spec()) for m in metas] + [(b, whole(b.shape)) for b in blocks]
    outs = [(sds((NX, 2, n * cap, width)), whole((NX, 2, n * cap, width)))]
    return call(body, pos, (1,), ins, outs, after=after)[0]


def combine(pos, metas, pieces, cots, cap, after=()):
    n, width = len(metas), pieces.shape[3]
    mixing = cots is not None

    def body(pos_ref, *refs):
        p = (pos_ref[0], pos_ref[1])
        pieces_in = refs[n]
        cots_in = refs[n + 1 : n + 1 + n] if mixing else ()
        outs = refs[len(refs) - n :]
        wide = [[pieces_in[k, e].astype(F32) for e in range(2)] for k in range(NX)]
        for i in range(n):
            tables, weights = slots(refs[i][...].astype(F32), p, cap)
            table = jnp.concatenate(tables, axis=0)
            rows = jnp.concatenate(
                [wide[k][e][i * cap : (i + 1) * cap] for k in range(NX) for e in range(2)], axis=0
            )
            rows16 = rows.astype(BF16)
            if mixing:
                scaled = jnp.concatenate([t * w for t, w in zip(tables, weights)], axis=0)
                high = scaled.astype(BF16)
                low = (scaled - high.astype(F32)).astype(BF16)
                total = dot(high, rows16, 0, 0) + dot(low, rows16, 0, 0)
                picked = dot(table.astype(BF16), cots_in[i][...], 1, 0)
                each = jnp.sum(picked * rows, axis=1, keepdims=True)
                grads = jnp.concatenate(
                    [
                        jnp.sum(t * each[q * cap : (q + 1) * cap], axis=0, keepdims=True)
                        for q, t in enumerate(tables)
                    ]
                    + [jnp.zeros((8 - 2 * NX, LANES), F32)] * (2 * NX < 8),
                    axis=0,
                )
            else:
                total = dot(table.astype(BF16), rows16, 0, 0)
            if i == 0:
                outs[i][0:LANES, :] = total
                if mixing:
                    outs[i][LANES : LANES + 8, 0:LANES] = grads
            else:
                outs[i][0:LANES, :] = total.astype(BF16)
                if mixing:
                    top = grads.astype(BF16)
                    outs[i][LANES : LANES + 16, :] = jnp.zeros((16, width), BF16)
                    outs[i][LANES : LANES + 16, 0:LANES] = jnp.concatenate(
                        [top.astype(F32), grads - top.astype(F32)], axis=0
                    ).astype(BF16)

    ins = [(m, meta_spec()) for m in metas] + [(pieces, whole(pieces.shape))]
    if mixing:
        ins += [(b, whole(b.shape)) for b in cots]
    outs = [sds((LANES + 8 * mixing, width), F32)]
    outs += [sds((LANES + 16 * mixing, width))] * (n - 1)
    outs = [(o, whole(o.shape)) for o in outs]
    return call(body, pos, (1,), ins, outs, after=after)


def weight_spec(w, across, other):
    rows, cols = w.shape[1], w.shape[2]
    half = (lambda pos: 1 - pos[3]) if other else (lambda pos: pos[3])
    if across:
        return pl.BlockSpec((1, rows // 2, cols), lambda e, pos: (e, half(pos), 0))
    return pl.BlockSpec((1, rows, cols // 2), lambda e, pos: (e, 0, half(pos)))


def partial_other(pos, pieces, mats, across, after):
    m, (_, _, part, width) = len(mats), pieces.shape
    rows = NX * part

    def body(pos_ref, *refs):
        rows_in, weights, (theirs, joined) = refs[0], refs[1 : 1 + m], refs[1 + m :]
        left = jnp.concatenate([rows_in[k, 0] for k in range(NX)], axis=0)
        joined[0] = left
        for i in range(m):
            out = dot(left, weights[i][0], 1, 1 if across else 0).astype(BF16)
            for y in range(NY):
                theirs[y, i, 0] = out[:, y * LANES : (y + 1) * LANES]

    ins = [(pieces, pl.BlockSpec((NX, 1, part, width), lambda e, pos: (0, e, 0, 0)))]
    ins += [(w, weight_spec(w, across, True)) for w in mats]
    outs = [
        (
            sds((NY, m, 2, rows, LANES)),
            pl.BlockSpec((NY, m, 1, rows, LANES), lambda e, pos: (0, 0, e, 0, 0)),
        ),
        (sds((2, rows, width)), pl.BlockSpec((1, rows, width), lambda e, pos: (e, 0, 0))),
    ]
    return call(body, pos, (2,), ins, outs, after=after)


def partial_own(pos, joined, mats, got, across, after):
    m, (_, rows, width) = len(mats), joined.shape

    def body(pos_ref, joined_ref, *refs):
        weights, got_ref, outs, hold = refs[:m], refs[m], refs[m + 1 : -1], refs[-1]
        for i in range(m):
            out = dot(joined_ref[0], weights[i][0], 1, 1 if across else 0)
            for y in range(NY):
                hold[y, i] = out[:, y * LANES : (y + 1) * LANES]
        for k in range(NY):
            at = lax.rem(pos_ref[2] + k, NY)
            for i in range(m):
                outs[k][i, 0] = (hold[at, i] + got_ref[at, i, 0].astype(F32)).astype(BF16)

    ins = [(joined, pl.BlockSpec((1, rows, width), lambda e, pos: (e, 0, 0)))]
    ins += [(w, weight_spec(w, across, False)) for w in mats]
    ins += [
        (got, pl.BlockSpec((NY, m, 1, rows, LANES), lambda e, pos: (0, 0, e, 0, 0))),
    ]
    outs = [
        (sds((m, 2, rows, LANES)), pl.BlockSpec((m, 1, rows, LANES), lambda e, pos: (0, e, 0, 0)))
        for _ in range(NY)
    ]
    scratch = [pltpu.VMEM((NY, m, rows, LANES), F32)]
    return call(body, pos, (2,), ins, outs, scratch, after=after)


def scattered(parts):
    return [parts[0]] + [lax.ppermute(parts[k], "tensor", y_shift(k)) for k in range(1, NY)]


def term_sum(refs, i):
    total = refs[0][i, 0].astype(F32)
    for r in refs[1:]:
        total = total + r[i, 0].astype(F32)
    return total


def sigmoid(v):
    return 1.0 / (1.0 + jnp.exp(-v))


def term_specs(terms):
    m, _, rows, _ = terms[0].shape
    spec = pl.BlockSpec((m, 1, rows, LANES), lambda e, pos: (0, e, 0, 0))
    return [(t, spec) for t in terms]


def activated(pos, terms, after):
    rows = terms[0].shape[2]

    def body(pos_ref, *refs):
        gate, up = term_sum(refs[:NY], 0), term_sum(refs[:NY], 1)
        refs[NY][0, 0] = (gate * sigmoid(gate) * up).astype(BF16)

    outs = [
        (
            sds((2, 1, rows, LANES)),
            pl.BlockSpec((1, 1, rows, LANES), lambda e, pos: (e, 0, 0, 0)),
        )
    ]
    return call(body, pos, (2,), term_specs(terms), outs, after=after)[0]


def differed(pos, terms, hid_terms, after):
    rows = terms[0].shape[2]

    def body(pos_ref, *refs):
        gate, up = term_sum(refs[:NY], 0), term_sum(refs[:NY], 1)
        hid = term_sum(refs[NY : 2 * NY], 0)
        s = sigmoid(gate)
        refs[2 * NY][0, 0] = (hid * up * s * (1.0 + gate * (1.0 - s))).astype(BF16)
        refs[2 * NY][0, 1] = (hid * (gate * s)).astype(BF16)

    outs = [
        (
            sds((2, 2, rows, LANES)),
            pl.BlockSpec((1, 2, rows, LANES), lambda e, pos: (e, 0, 0, 0)),
        )
    ]
    ins = term_specs(terms) + term_specs(hid_terms)
    return call(body, pos, (2,), ins, outs, after=after)[0]


def gathered(own):
    return [own] + [lax.ppermute(own, "tensor", y_shift(k)) for k in range(1, NY)]


def products(pos, mine, others, mats, across, part, after):
    rows = mine[0].shape[2]
    m, hidden = len(mats), 2 * NY * LANES
    width = mats[0].shape[1] if across else mats[0].shape[2]

    def body(pos_ref, *refs):
        ins, other, weights = refs[:NY], refs[NY], refs[NY + 1 : NY + 1 + m]
        outs, fulls = refs[NY + 1 + m], refs[NY + 2 + m :]
        y, c = pos_ref[2], pos_ref[3]
        total = None
        for i in range(m):
            for k in range(NY):
                behind = lax.rem(y + NY - k, NY)
                at = pl.multiple_of((c * NY + behind) * LANES, LANES)
                fulls[i][0, :, pl.ds(at, LANES)] = ins[k][0, i]
                at = pl.multiple_of(((1 - c) * NY + behind) * LANES, LANES)
                fulls[i][0, :, pl.ds(at, LANES)] = other[k, 0, i]
            term = dot(fulls[i][0], weights[i][0], 1, 1 if across else 0)
            total = term if total is None else total + term
        total = total.astype(BF16)
        for k in range(NX):
            outs[k, 0] = total[k * part : (k + 1) * part]

    ins = [(s, pl.BlockSpec((1, m, rows, LANES), lambda e, pos: (e, 0, 0, 0))) for s in mine]
    ins += [(others, pl.BlockSpec((NY, 1, m, rows, LANES), lambda e, pos: (0, e, 0, 0, 0)))]
    ins += [(w, pl.BlockSpec((1,) + w.shape[1:], lambda e, pos: (e, 0, 0))) for w in mats]
    outs = [
        (
            sds((NX, 2, part, width)),
            pl.BlockSpec((NX, 1, part, width), lambda e, pos: (0, e, 0, 0)),
        )
    ]
    outs += [
        (sds((2, rows, hidden)), pl.BlockSpec((1, rows, hidden), lambda e, pos: (e, 0, 0)))
        for _ in range(m)
    ]
    got = call(body, pos, (2,), ins, outs, after=after)
    return got[0], got[1:]


def weight_grad(pos, left, right, left_wide, after):
    rows, a, b = left.shape[1], left.shape[2], right.shape[2]
    ba, bb = (a // 2, b) if left_wide else (a, b // 2)

    def body(pos_ref, left_ref, right_ref, out):
        out[0] = dot(left_ref[0], right_ref[0], 0, 0).astype(BF16)

    def spec(size, cut):
        return pl.BlockSpec((1, rows, size), lambda e, h, pos: (e, 0, h if cut else 0))

    ins = [(left, spec(ba, left_wide)), (right, spec(bb, not left_wide))]
    out = pl.BlockSpec(
        (1, ba, bb), lambda e, h, pos: (e, h if left_wide else 0, 0 if left_wide else h)
    )
    return call(body, pos, (2, 2), ins, [(sds((2, a, b)), out)], after=after)[0]


def exchanged(pieces):
    return lax.all_to_all(pieces, "expert", 0, 0, axis_index_groups=x_groups(), tiled=True)


def ring(own):
    block = {0: own}
    for j in range(1, NZ // 2 + 1):
        block[j] = lax.ppermute(block[j - 1], "expert", z_shift(1))
        if j < NZ // 2:
            block[NZ - j] = lax.ppermute(block[(NZ - j + 1) % NZ], "expert", z_shift(-1))
    return [block[j] for j in range(NZ)]


def returned(values):
    return [values[0]] + [lax.ppermute(values[j], "expert", z_shift(-j)) for j in range(1, NZ)]


def order(value, *after):
    return lax.optimization_barrier((value, after))[0]


def per_device(
    tokens, expert_ids, combine_weight, gate_weight, up_weight, down_weight, out_cotangent
):
    tok_rows, width = tokens.shape
    top_count = expert_ids.shape[1]
    cap = 3 * tok_rows * top_count // (2 * gate_weight.shape[0] * NZ * NX)
    group, share = lax.axis_index("expert"), lax.axis_index("tensor")
    pos = jnp.stack([group // NX, group % NX, share // 2, share % 2]).astype(jnp.int32)

    ids = expert_ids.T
    weight = combine_weight.T
    high = lax.reduce_precision(weight, 8, 7)
    middle = lax.reduce_precision(weight - high, 8, 7)
    low = weight - high - middle
    meta = jnp.concatenate([ids.astype(F32), high, middle, low], axis=1).astype(BF16)
    meta = jnp.pad(meta, ((0, 16 - top_count), (0, width - 4 * tok_rows)))
    part = NZ * cap

    toks = ring(jnp.concatenate([tokens, meta], axis=0))
    cots = ring(out_cotangent)
    far = NZ // 2
    rows = exchanged(dispatch(pos, toks, toks, cap, False, [cots[far], cots[far + 1]]))
    theirs, routed = partial_other(pos, rows, [gate_weight, up_weight], False, [])
    sent = dispatch(pos, toks, cots, cap, True, [theirs])
    parts = partial_own(
        pos, routed, [gate_weight, up_weight], lax.ppermute(theirs, "tensor", flip(1)), False, [sent]
    )
    terms = scattered(parts)
    acts = gathered(activated(pos, terms, []))
    theirs, cotangents = partial_other(pos, exchanged(sent), [down_weight], True, acts[1::2])
    parts = partial_own(
        pos, cotangents, [down_weight], lax.ppermute(theirs, "tensor", flip(1)), True, []
    )
    hid_terms = scattered(parts)
    others = lax.ppermute(jnp.stack(acts), "tensor", flip(1))
    out, (act_full,) = products(pos, acts, others, [down_weight], False, part, [parts[0]])
    diffs = gathered(differed(pos, terms, hid_terms, [out]))
    back = exchanged(out)
    sums = combine(pos, toks, back, cots, cap)
    mixed_parts = returned(sums)
    others = lax.ppermute(jnp.stack(order(diffs, sums[0])), "tensor", flip(1))
    out, (gate_full, up_full) = products(
        pos, diffs, others, [gate_weight, up_weight], True, part, [sums[0]]
    )
    back = exchanged(out)
    down_grad = weight_grad(pos, act_full, cotangents, True, [out])
    late = order(mixed_parts, down_grad)
    gate_grad = weight_grad(pos, routed, gate_full, False, [])
    up_grad = weight_grad(pos, routed, up_full, False, [])

    grads = jnp.zeros(ids.shape, F32)
    for j in range(NZ):
        table = late[j][tok_rows : tok_rows + 8, :LANES].astype(F32)
        if j:
            table = table + late[j][tok_rows + 8 :, :LANES].astype(F32)
        for k in range(NX):
            for e in range(2):
                expert = ((pos[0] + j) % NZ * NX + k) * 2 + e
                grads = grads + jnp.where(ids == expert, table[k * 2 + e][None, :], 0.0)
    grads = grads + lax.ppermute(grads, "tensor", flip(1))
    far1, far2, far3 = [lax.ppermute(grads, "tensor", flip(m)) for m in (2, 4, 6)]
    grads = (grads + far1) + (far2 + far3)

    done = [gate_grad, up_grad, grads]
    grad_parts = returned(combine(pos, toks, back, None, cap, done))
    mixed = sum(v[:tok_rows].astype(F32) for v in late).astype(BF16)
    token_grad = sum(v.astype(F32) for v in grad_parts).astype(BF16)
    return (mixed, token_grad, grads.T, gate_grad, up_grad, down_grad)


def solution(mesh):
    placed = (
        P("expert", "tensor"),
        P("expert", None),
        P("expert", None),
        P("expert", "tensor", None),
        P("expert", "tensor", None),
        P("expert", None, "tensor"),
        P("expert", "tensor"),
    )
    return jax.shard_map(
        per_device,
        mesh=mesh,
        in_specs=placed,
        out_specs=(
            P("expert", "tensor"),
            P("expert", "tensor"),
            P("expert", None),
            P("expert", "tensor", None),
            P("expert", "tensor", None),
            P("expert", None, "tensor"),
        ),
        check_vma=False,
    )
```

```python
import jax
import jax.numpy as jnp
from jax import lax
from jax.experimental import pallas as pl
from jax.experimental.pallas import tpu as pltpu
from jax.sharding import PartitionSpec as P

NZ, NX, NY = 8, 4, 4
LANES = 128
F32, BF16 = jnp.float32, jnp.bfloat16


def z_shift(k):
    return [(z * NX + x, (z + k) % NZ * NX + x) for z in range(NZ) for x in range(NX)]


def x_groups():
    return [[z * NX + x for x in range(NX)] for z in range(NZ)]


def y_shift(k):
    return [(y * 2 + c, (y + k) % NY * 2 + c) for y in range(NY) for c in range(2)]


def flip(mask):
    return [(i, i ^ mask) for i in range(NY * 2)]


def call(body, pos, grid, ins, outs, scratch=(), flops=0, after=()):
    first, extra = len(ins), len(after)
    ins = list(ins) + [(a, pl.BlockSpec(memory_space=pl.ANY)) for a in after]
    arrays = [a for a, _ in ins]
    inner = body

    def body(pos_ref, *refs):
        inner(pos_ref, *refs[:first], *refs[first + extra :])

    moved = sum(a.size * a.dtype.itemsize for a in arrays[:first]) + sum(
        s.size * s.dtype.itemsize for s, _ in outs
    )
    return pl.pallas_call(
        body,
        out_shape=[s for s, _ in outs],
        grid_spec=pltpu.PrefetchScalarGridSpec(
            num_scalar_prefetch=1,
            grid=grid,
            in_specs=[s for _, s in ins],
            out_specs=[s for _, s in outs],
            scratch_shapes=list(scratch),
        ),
        compiler_params=pltpu.CompilerParams(vmem_limit_bytes=56 << 20),
        cost_estimate=pl.CostEstimate(flops=1, bytes_accessed=1, transcendentals=0),
    )(pos, *arrays)


def whole(shape):
    return pl.BlockSpec(shape, lambda i, pos: (0,) * len(shape))


def sds(shape, dtype=BF16):
    return jax.ShapeDtypeStruct(shape, dtype)


def dot(a, b, ca, cb):
    return lax.dot_general(a, b, (((ca,), (cb,)), ((), ())), preferred_element_type=F32)


def triangle():
    rows = lax.broadcasted_iota(jnp.int32, (LANES, LANES), 0)
    cols = lax.broadcasted_iota(jnp.int32, (LANES, LANES), 1)
    return jnp.where(rows < cols, 1.0, 0.0).astype(BF16)


def slots(meta, pos, cap):
    ids = meta[:8, :LANES]
    weight = meta[:8, LANES : 2 * LANES] + meta[:8, 2 * LANES : 3 * LANES] + meta[:8, 3 * LANES :]
    named, weights = [], []
    for k in range(NX):
        for e in range(2):
            expert = (pos[0] * NX + k) * 2 + e
            hit = ids == expert.astype(F32)
            named.append(jnp.sum(jnp.where(hit, 1.0, 0.0), axis=0, keepdims=True))
            weights.append(jnp.sum(jnp.where(hit, weight, 0.0), axis=0, keepdims=True))
    all_named = jnp.concatenate(named, axis=0)
    place = dot(all_named.astype(BF16), triangle(), 1, 0)
    place = jnp.where(all_named > 0.5, place, -1.0)
    count = lax.broadcasted_iota(jnp.int32, (cap, LANES), 0).astype(F32)
    tables = [jnp.where(count == place[q : q + 1], 1.0, 0.0) for q in range(2 * NX)]
    return tables, weights


def meta_spec():
    return pl.BlockSpec((16, 4 * LANES), lambda i, pos: (LANES // 16, 0))


def dispatch(pos, metas, blocks, cap, weighted, after=()):
    n, width = len(metas), blocks[0].shape[1]

    def body(pos_ref, *refs):
        p = (pos_ref[0], pos_ref[1])
        rows = []
        for i in range(n):
            tables, weights = slots(refs[i][...].astype(F32), p, cap)
            table = jnp.concatenate(tables, axis=0)
            taken = dot(table.astype(BF16), refs[n + i][0:LANES, :], 1, 0)
            if weighted:
                scale = jnp.concatenate(
                    [jnp.sum(t * w, axis=1, keepdims=True) for t, w in zip(tables, weights)], axis=0
                )
                taken = taken * scale
            rows.append(taken)
        for k in range(NX):
            for e in range(2):
                at = (k * 2 + e) * cap
                refs[2 * n][k, e] = jnp.concatenate(
                    [r[at : at + cap] for r in rows], axis=0
                ).astype(BF16)

    ins = [(m, meta_spec()) for m in metas] + [(b, whole(b.shape)) for b in blocks]
    outs = [(sds((NX, 2, n * cap, width)), whole((NX, 2, n * cap, width)))]
    return call(body, pos, (1,), ins, outs, after=after)[0]


def combine(pos, metas, pieces, cots, cap, after=()):
    n, width = len(metas), pieces.shape[3]
    mixing = cots is not None

    def body(pos_ref, *refs):
        p = (pos_ref[0], pos_ref[1])
        pieces_in = refs[n]
        cots_in = refs[n + 1 : n + 1 + n] if mixing else ()
        outs = refs[len(refs) - n :]
        wide = [[pieces_in[k, e].astype(F32) for e in range(2)] for k in range(NX)]
        for i in range(n):
            tables, weights = slots(refs[i][...].astype(F32), p, cap)
            table = jnp.concatenate(tables, axis=0)
            rows = jnp.concatenate(
                [wide[k][e][i * cap : (i + 1) * cap] for k in range(NX) for e in range(2)], axis=0
            )
            rows16 = rows.astype(BF16)
            if mixing:
                scaled = jnp.concatenate([t * w for t, w in zip(tables, weights)], axis=0)
                high = scaled.astype(BF16)
                low = (scaled - high.astype(F32)).astype(BF16)
                total = dot(high, rows16, 0, 0) + dot(low, rows16, 0, 0)
                picked = dot(table.astype(BF16), cots_in[i][...], 1, 0)
                each = jnp.sum(picked * rows, axis=1, keepdims=True)
                grads = jnp.concatenate(
                    [
                        jnp.sum(t * each[q * cap : (q + 1) * cap], axis=0, keepdims=True)
                        for q, t in enumerate(tables)
                    ]
                    + [jnp.zeros((8 - 2 * NX, LANES), F32)] * (2 * NX < 8),
                    axis=0,
                )
            else:
                total = dot(table.astype(BF16), rows16, 0, 0)
            if i == 0:
                outs[i][0:LANES, :] = total
                if mixing:
                    outs[i][LANES : LANES + 8, 0:LANES] = grads
            else:
                outs[i][0:LANES, :] = total.astype(BF16)
                if mixing:
                    top = grads.astype(BF16)
                    outs[i][LANES : LANES + 16, :] = jnp.zeros((16, width), BF16)
                    outs[i][LANES : LANES + 16, 0:LANES] = jnp.concatenate(
                        [top.astype(F32), grads - top.astype(F32)], axis=0
                    ).astype(BF16)

    ins = [(m, meta_spec()) for m in metas] + [(pieces, whole(pieces.shape))]
    if mixing:
        ins += [(b, whole(b.shape)) for b in cots]
    outs = [sds((LANES + 8 * mixing, width), F32)]
    outs += [sds((LANES + 16 * mixing, width))] * (n - 1)
    outs = [(o, whole(o.shape)) for o in outs]
    return call(body, pos, (1,), ins, outs, after=after)


def weight_spec(w, across, other):
    rows, cols = w.shape[1], w.shape[2]
    half = (lambda pos: 1 - pos[3]) if other else (lambda pos: pos[3])
    if across:
        return pl.BlockSpec((1, rows // 2, cols), lambda e, pos: (e, half(pos), 0))
    return pl.BlockSpec((1, rows, cols // 2), lambda e, pos: (e, 0, half(pos)))


def partial_other(pos, pieces, mats, across, after):
    m, (_, _, part, width) = len(mats), pieces.shape
    rows = NX * part

    def body(pos_ref, *refs):
        rows_in, weights, (theirs, joined) = refs[0], refs[1 : 1 + m], refs[1 + m :]
        left = jnp.concatenate([rows_in[k, 0] for k in range(NX)], axis=0)
        joined[0] = left
        for i in range(m):
            out = dot(left, weights[i][0], 1, 1 if across else 0).astype(BF16)
            for y in range(NY):
                theirs[y, i, 0] = out[:, y * LANES : (y + 1) * LANES]

    ins = [(pieces, pl.BlockSpec((NX, 1, part, width), lambda e, pos: (0, e, 0, 0)))]
    ins += [(w, weight_spec(w, across, True)) for w in mats]
    outs = [
        (
            sds((NY, m, 2, rows, LANES)),
            pl.BlockSpec((NY, m, 1, rows, LANES), lambda e, pos: (0, 0, e, 0, 0)),
        ),
        (sds((2, rows, width)), pl.BlockSpec((1, rows, width), lambda e, pos: (e, 0, 0))),
    ]
    return call(body, pos, (2,), ins, outs, after=after)


def partial_own(pos, joined, mats, got, across, after):
    m, (_, rows, width) = len(mats), joined.shape

    def body(pos_ref, joined_ref, *refs):
        weights, got_ref, outs, hold = refs[:m], refs[m], refs[m + 1 : -1], refs[-1]
        for i in range(m):
            out = dot(joined_ref[0], weights[i][0], 1, 1 if across else 0)
            for y in range(NY):
                hold[y, i] = out[:, y * LANES : (y + 1) * LANES]
        for k in range(NY):
            at = lax.rem(pos_ref[2] + k, NY)
            for i in range(m):
                outs[k][i, 0] = (hold[at, i] + got_ref[at, i, 0].astype(F32)).astype(BF16)

    ins = [(joined, pl.BlockSpec((1, rows, width), lambda e, pos: (e, 0, 0)))]
    ins += [(w, weight_spec(w, across, False)) for w in mats]
    ins += [
        (got, pl.BlockSpec((NY, m, 1, rows, LANES), lambda e, pos: (0, 0, e, 0, 0))),
    ]
    outs = [
        (sds((m, 2, rows, LANES)), pl.BlockSpec((m, 1, rows, LANES), lambda e, pos: (0, e, 0, 0)))
        for _ in range(NY)
    ]
    scratch = [pltpu.VMEM((NY, m, rows, LANES), F32)]
    return call(body, pos, (2,), ins, outs, scratch, after=after)


def scattered(parts):
    return [parts[0]] + [lax.ppermute(parts[k], "tensor", y_shift(k)) for k in range(1, NY)]


def term_sum(refs, i):
    total = refs[0][i, 0].astype(F32)
    for r in refs[1:]:
        total = total + r[i, 0].astype(F32)
    return total


def sigmoid(v):
    return 1.0 / (1.0 + jnp.exp(-v))


def term_specs(terms):
    m, _, rows, _ = terms[0].shape
    spec = pl.BlockSpec((m, 1, rows, LANES), lambda e, pos: (0, e, 0, 0))
    return [(t, spec) for t in terms]


def activated(pos, terms, after):
    rows = terms[0].shape[2]

    def body(pos_ref, *refs):
        gate, up = term_sum(refs[:NY], 0), term_sum(refs[:NY], 1)
        refs[NY][0, 0] = (gate * sigmoid(gate) * up).astype(BF16)

    outs = [
        (
            sds((2, 1, rows, LANES)),
            pl.BlockSpec((1, 1, rows, LANES), lambda e, pos: (e, 0, 0, 0)),
        )
    ]
    return call(body, pos, (2,), term_specs(terms), outs, after=after)[0]


def differed(pos, terms, hid_terms, after):
    rows = terms[0].shape[2]

    def body(pos_ref, *refs):
        gate, up = term_sum(refs[:NY], 0), term_sum(refs[:NY], 1)
        hid = term_sum(refs[NY : 2 * NY], 0)
        s = sigmoid(gate)
        refs[2 * NY][0, 0] = (hid * up * s * (1.0 + gate * (1.0 - s))).astype(BF16)
        refs[2 * NY][0, 1] = (hid * (gate * s)).astype(BF16)

    outs = [
        (
            sds((2, 2, rows, LANES)),
            pl.BlockSpec((1, 2, rows, LANES), lambda e, pos: (e, 0, 0, 0)),
        )
    ]
    ins = term_specs(terms) + term_specs(hid_terms)
    return call(body, pos, (2,), ins, outs, after=after)[0]


def gathered(own):
    return [own] + [lax.ppermute(own, "tensor", y_shift(k)) for k in range(1, NY)]


def products(pos, mine, others, mats, across, part, after):
    rows = mine[0].shape[2]
    m, hidden = len(mats), 2 * NY * LANES
    width = mats[0].shape[1] if across else mats[0].shape[2]

    def body(pos_ref, *refs):
        ins, other, weights = refs[:NY], refs[NY], refs[NY + 1 : NY + 1 + m]
        outs, fulls = refs[NY + 1 + m], refs[NY + 2 + m :]
        y, c = pos_ref[2], pos_ref[3]
        total = None
        for i in range(m):
            for k in range(NY):
                behind = lax.rem(y + NY - k, NY)
                at = pl.multiple_of((c * NY + behind) * LANES, LANES)
                fulls[i][0, :, pl.ds(at, LANES)] = ins[k][0, i]
                at = pl.multiple_of(((1 - c) * NY + behind) * LANES, LANES)
                fulls[i][0, :, pl.ds(at, LANES)] = other[k, 0, i]
            term = dot(fulls[i][0], weights[i][0], 1, 1 if across else 0)
            total = term if total is None else total + term
        total = total.astype(BF16)
        for k in range(NX):
            outs[k, 0] = total[k * part : (k + 1) * part]

    ins = [(s, pl.BlockSpec((1, m, rows, LANES), lambda e, pos: (e, 0, 0, 0))) for s in mine]
    ins += [(others, pl.BlockSpec((NY, 1, m, rows, LANES), lambda e, pos: (0, e, 0, 0, 0)))]
    ins += [(w, pl.BlockSpec((1,) + w.shape[1:], lambda e, pos: (e, 0, 0))) for w in mats]
    outs = [
        (
            sds((NX, 2, part, width)),
            pl.BlockSpec((NX, 1, part, width), lambda e, pos: (0, e, 0, 0)),
        )
    ]
    outs += [
        (sds((2, rows, hidden)), pl.BlockSpec((1, rows, hidden), lambda e, pos: (e, 0, 0)))
        for _ in range(m)
    ]
    got = call(body, pos, (2,), ins, outs, after=after)
    return got[0], got[1:]


def weight_grad(pos, left, right, left_wide, after):
    rows, a, b = left.shape[1], left.shape[2], right.shape[2]
    ba, bb = (a // 2, b) if left_wide else (a, b // 2)

    def body(pos_ref, left_ref, right_ref, out):
        out[0] = dot(left_ref[0], right_ref[0], 0, 0).astype(BF16)

    def spec(size, cut):
        return pl.BlockSpec((1, rows, size), lambda e, h, pos: (e, 0, h if cut else 0))

    ins = [(left, spec(ba, left_wide)), (right, spec(bb, not left_wide))]
    out = pl.BlockSpec(
        (1, ba, bb), lambda e, h, pos: (e, h if left_wide else 0, 0 if left_wide else h)
    )
    return call(body, pos, (2, 2), ins, [(sds((2, a, b)), out)], after=after)[0]


def exchanged(pieces):
    return lax.all_to_all(pieces, "expert", 0, 0, axis_index_groups=x_groups(), tiled=True)


def ring(own):
    block = {0: own}
    for j in range(1, NZ // 2 + 1):
        block[j] = lax.ppermute(block[j - 1], "expert", z_shift(1))
        if j < NZ // 2:
            block[NZ - j] = lax.ppermute(block[(NZ - j + 1) % NZ], "expert", z_shift(-1))
    return [block[j] for j in range(NZ)]


def returned(values):
    return [values[0]] + [lax.ppermute(values[j], "expert", z_shift(-j)) for j in range(1, NZ)]


def order(value, *after):
    return lax.optimization_barrier((value, after))[0]


def per_device(
    tokens, expert_ids, combine_weight, gate_weight, up_weight, down_weight, out_cotangent
):
    tok_rows, width = tokens.shape
    top_count = expert_ids.shape[1]
    cap = 3 * tok_rows * top_count // (2 * gate_weight.shape[0] * NZ * NX)
    group, share = lax.axis_index("expert"), lax.axis_index("tensor")
    pos = jnp.stack([group // NX, group % NX, share // 2, share % 2]).astype(jnp.int32)

    ids = expert_ids.T
    weight = combine_weight.T
    high = lax.reduce_precision(weight, 8, 7)
    middle = lax.reduce_precision(weight - high, 8, 7)
    low = weight - high - middle
    meta = jnp.concatenate([ids.astype(F32), high, middle, low], axis=1).astype(BF16)
    meta = jnp.pad(meta, ((0, 16 - top_count), (0, width - 4 * tok_rows)))
    part = NZ * cap

    toks = ring(jnp.concatenate([tokens, meta], axis=0))
    cots = ring(out_cotangent)
    far = NZ // 2
    rows = exchanged(dispatch(pos, toks, toks, cap, False, [cots[far], cots[far + 1]]))
    theirs, routed = partial_other(pos, rows, [gate_weight, up_weight], False, [])
    sent = dispatch(pos, toks, cots, cap, True, [theirs])
    parts = partial_own(
        pos, routed, [gate_weight, up_weight], lax.ppermute(theirs, "tensor", flip(1)), False, [sent]
    )
    terms = scattered(parts)
    act = activated(pos, terms, [])
    acts = gathered(act)
    theirs, cotangents = partial_other(pos, exchanged(sent), [down_weight], True, [act])
    parts = partial_own(
        pos, cotangents, [down_weight], lax.ppermute(theirs, "tensor", flip(1)), True, []
    )
    hid_terms = scattered(parts)
    others = lax.ppermute(jnp.stack(acts), "tensor", flip(1))
    out, (act_full,) = products(pos, acts, others, [down_weight], False, part, [parts[0]])
    diffs = gathered(differed(pos, terms, hid_terms, [out]))
    back = exchanged(out)
    sums = combine(pos, toks, back, cots, cap)
    mixed_parts = returned(sums)
    down_grad = weight_grad(pos, act_full, cotangents, True, [sums[0]])
    early = [mixed_parts[j] for j in (1, 2, NZ - 2, NZ - 1)]
    others = lax.ppermute(jnp.stack(order(diffs, down_grad, *early)), "tensor", flip(1))
    out, (gate_full, up_full) = products(
        pos, diffs, others, [gate_weight, up_weight], True, part, [sums[0]]
    )
    back = exchanged(out)
    late = order(mixed_parts, out)
    gate_grad = weight_grad(pos, routed, gate_full, False, [])
    up_grad = weight_grad(pos, routed, up_full, False, [])

    grads = jnp.zeros(ids.shape, F32)
    for j in range(NZ):
        table = late[j][tok_rows : tok_rows + 8, :LANES].astype(F32)
        if j:
            table = table + late[j][tok_rows + 8 :, :LANES].astype(F32)
        for k in range(NX):
            for e in range(2):
                expert = ((pos[0] + j) % NZ * NX + k) * 2 + e
                grads = grads + jnp.where(ids == expert, table[k * 2 + e][None, :], 0.0)
    grads = grads + lax.ppermute(grads, "tensor", flip(1))
    far1, far2, far3 = [lax.ppermute(grads, "tensor", flip(m)) for m in (2, 4, 6)]
    grads = (grads + far1) + (far2 + far3)

    done = [gate_grad, up_grad, grads]
    grad_parts = returned(combine(pos, toks, back, None, cap, done))
    mixed = sum(v[:tok_rows].astype(F32) for v in late).astype(BF16)
    token_grad = sum(v.astype(F32) for v in grad_parts).astype(BF16)
    return (mixed, token_grad, grads.T, gate_grad, up_grad, down_grad)


def solution(mesh):
    placed = (
        P("expert", "tensor"),
        P("expert", None),
        P("expert", None),
        P("expert", "tensor", None),
        P("expert", "tensor", None),
        P("expert", None, "tensor"),
        P("expert", "tensor"),
    )
    return jax.shard_map(
        per_device,
        mesh=mesh,
        in_specs=placed,
        out_specs=(
            P("expert", "tensor"),
            P("expert", "tensor"),
            P("expert", None),
            P("expert", "tensor", None),
            P("expert", "tensor", None),
            P("expert", None, "tensor"),
        ),
        check_vma=False,
    )
```

```python
import jax
import jax.numpy as jnp
from jax import lax
from jax.experimental import pallas as pl
from jax.experimental.pallas import tpu as pltpu
from jax.sharding import PartitionSpec as P

NZ, NX, NY = 8, 4, 4
LANES = 128
F32, BF16 = jnp.float32, jnp.bfloat16


def z_shift(k):
    return [(z * NX + x, (z + k) % NZ * NX + x) for z in range(NZ) for x in range(NX)]


def x_groups():
    return [[z * NX + x for x in range(NX)] for z in range(NZ)]


def y_shift(k):
    return [(y * 2 + c, (y + k) % NY * 2 + c) for y in range(NY) for c in range(2)]


def flip(mask):
    return [(i, i ^ mask) for i in range(NY * 2)]


def call(body, pos, grid, ins, outs, scratch=(), flops=0, after=()):
    first, extra = len(ins), len(after)
    ins = list(ins) + [(a, pl.BlockSpec(memory_space=pl.ANY)) for a in after]
    arrays = [a for a, _ in ins]
    inner = body

    def body(pos_ref, *refs):
        inner(pos_ref, *refs[:first], *refs[first + extra :])

    moved = sum(a.size * a.dtype.itemsize for a in arrays[:first]) + sum(
        s.size * s.dtype.itemsize for s, _ in outs
    )
    return pl.pallas_call(
        body,
        out_shape=[s for s, _ in outs],
        grid_spec=pltpu.PrefetchScalarGridSpec(
            num_scalar_prefetch=1,
            grid=grid,
            in_specs=[s for _, s in ins],
            out_specs=[s for _, s in outs],
            scratch_shapes=list(scratch),
        ),
        compiler_params=pltpu.CompilerParams(vmem_limit_bytes=56 << 20),
        cost_estimate=pl.CostEstimate(flops=1, bytes_accessed=1, transcendentals=0),
    )(pos, *arrays)


def whole(shape):
    return pl.BlockSpec(shape, lambda i, pos: (0,) * len(shape))


def sds(shape, dtype=BF16):
    return jax.ShapeDtypeStruct(shape, dtype)


def dot(a, b, ca, cb):
    return lax.dot_general(a, b, (((ca,), (cb,)), ((), ())), preferred_element_type=F32)


def triangle():
    rows = lax.broadcasted_iota(jnp.int32, (LANES, LANES), 0)
    cols = lax.broadcasted_iota(jnp.int32, (LANES, LANES), 1)
    return jnp.where(rows < cols, 1.0, 0.0).astype(BF16)


def slots(meta, pos, cap):
    ids = meta[:8, :LANES]
    weight = meta[:8, LANES : 2 * LANES] + meta[:8, 2 * LANES : 3 * LANES] + meta[:8, 3 * LANES :]
    named, weights = [], []
    for k in range(NX):
        for e in range(2):
            expert = (pos[0] * NX + k) * 2 + e
            hit = ids == expert.astype(F32)
            named.append(jnp.sum(jnp.where(hit, 1.0, 0.0), axis=0, keepdims=True))
            weights.append(jnp.sum(jnp.where(hit, weight, 0.0), axis=0, keepdims=True))
    all_named = jnp.concatenate(named, axis=0)
    place = dot(all_named.astype(BF16), triangle(), 1, 0)
    place = jnp.where(all_named > 0.5, place, -1.0)
    count = lax.broadcasted_iota(jnp.int32, (cap, LANES), 0).astype(F32)
    tables = [jnp.where(count == place[q : q + 1], 1.0, 0.0) for q in range(2 * NX)]
    return tables, weights


def meta_spec():
    return pl.BlockSpec((16, 4 * LANES), lambda i, pos: (LANES // 16, 0))


def dispatch(pos, metas, blocks, cap, weighted, after=()):
    n, width = len(metas), blocks[0].shape[1]

    def body(pos_ref, *refs):
        p = (pos_ref[0], pos_ref[1])
        rows = []
        for i in range(n):
            tables, weights = slots(refs[i][...].astype(F32), p, cap)
            table = jnp.concatenate(tables, axis=0)
            taken = dot(table.astype(BF16), refs[n + i][0:LANES, :], 1, 0)
            if weighted:
                scale = jnp.concatenate(
                    [jnp.sum(t * w, axis=1, keepdims=True) for t, w in zip(tables, weights)], axis=0
                )
                taken = taken * scale
            rows.append(taken)
        for k in range(NX):
            for e in range(2):
                at = (k * 2 + e) * cap
                refs[2 * n][k, e] = jnp.concatenate(
                    [r[at : at + cap] for r in rows], axis=0
                ).astype(BF16)

    ins = [(m, meta_spec()) for m in metas] + [(b, whole(b.shape)) for b in blocks]
    outs = [(sds((NX, 2, n * cap, width)), whole((NX, 2, n * cap, width)))]
    return call(body, pos, (1,), ins, outs, after=after)[0]


def combine(pos, metas, pieces, cots, cap, after=()):
    n, width = len(metas), pieces.shape[3]
    mixing = cots is not None

    def body(pos_ref, *refs):
        p = (pos_ref[0], pos_ref[1])
        pieces_in = refs[n]
        cots_in = refs[n + 1 : n + 1 + n] if mixing else ()
        outs = refs[len(refs) - n :]
        wide = [[pieces_in[k, e].astype(F32) for e in range(2)] for k in range(NX)]
        for i in range(n):
            tables, weights = slots(refs[i][...].astype(F32), p, cap)
            table = jnp.concatenate(tables, axis=0)
            rows = jnp.concatenate(
                [wide[k][e][i * cap : (i + 1) * cap] for k in range(NX) for e in range(2)], axis=0
            )
            rows16 = rows.astype(BF16)
            if mixing:
                scaled = jnp.concatenate([t * w for t, w in zip(tables, weights)], axis=0)
                high = scaled.astype(BF16)
                low = (scaled - high.astype(F32)).astype(BF16)
                total = dot(high, rows16, 0, 0) + dot(low, rows16, 0, 0)
                picked = dot(table.astype(BF16), cots_in[i][...], 1, 0)
                each = jnp.sum(picked * rows, axis=1, keepdims=True)
                grads = jnp.concatenate(
                    [
                        jnp.sum(t * each[q * cap : (q + 1) * cap], axis=0, keepdims=True)
                        for q, t in enumerate(tables)
                    ]
                    + [jnp.zeros((8 - 2 * NX, LANES), F32)] * (2 * NX < 8),
                    axis=0,
                )
            else:
                total = dot(table.astype(BF16), rows16, 0, 0)
            if i == 0:
                outs[i][0:LANES, :] = total
                if mixing:
                    outs[i][LANES : LANES + 8, 0:LANES] = grads
            else:
                outs[i][0:LANES, :] = total.astype(BF16)
                if mixing:
                    top = grads.astype(BF16)
                    outs[i][LANES : LANES + 16, :] = jnp.zeros((16, width), BF16)
                    outs[i][LANES : LANES + 16, 0:LANES] = jnp.concatenate(
                        [top.astype(F32), grads - top.astype(F32)], axis=0
                    ).astype(BF16)

    ins = [(m, meta_spec()) for m in metas] + [(pieces, whole(pieces.shape))]
    if mixing:
        ins += [(b, whole(b.shape)) for b in cots]
    outs = [sds((LANES + 8 * mixing, width), F32)]
    outs += [sds((LANES + 16 * mixing, width))] * (n - 1)
    outs = [(o, whole(o.shape)) for o in outs]
    return call(body, pos, (1,), ins, outs, after=after)


def weight_spec(w, across, other):
    rows, cols = w.shape[1], w.shape[2]
    half = (lambda pos: 1 - pos[3]) if other else (lambda pos: pos[3])
    if across:
        return pl.BlockSpec((1, rows // 2, cols), lambda e, pos: (e, half(pos), 0))
    return pl.BlockSpec((1, rows, cols // 2), lambda e, pos: (e, 0, half(pos)))


def partial_other(pos, pieces, mats, across, after):
    m, (_, _, part, width) = len(mats), pieces.shape
    rows = NX * part

    def body(pos_ref, *refs):
        rows_in, weights, (theirs, joined) = refs[0], refs[1 : 1 + m], refs[1 + m :]
        left = jnp.concatenate([rows_in[k, 0] for k in range(NX)], axis=0)
        joined[0] = left
        for i in range(m):
            out = dot(left, weights[i][0], 1, 1 if across else 0).astype(BF16)
            for y in range(NY):
                theirs[y, i, 0] = out[:, y * LANES : (y + 1) * LANES]

    ins = [(pieces, pl.BlockSpec((NX, 1, part, width), lambda e, pos: (0, e, 0, 0)))]
    ins += [(w, weight_spec(w, across, True)) for w in mats]
    outs = [
        (
            sds((NY, m, 2, rows, LANES)),
            pl.BlockSpec((NY, m, 1, rows, LANES), lambda e, pos: (0, 0, e, 0, 0)),
        ),
        (sds((2, rows, width)), pl.BlockSpec((1, rows, width), lambda e, pos: (e, 0, 0))),
    ]
    return call(body, pos, (2,), ins, outs, after=after)


def partial_own(pos, joined, mats, got, across, after):
    m, (_, rows, width) = len(mats), joined.shape

    def body(pos_ref, joined_ref, *refs):
        weights, got_ref, outs, hold = refs[:m], refs[m], refs[m + 1 : -1], refs[-1]
        for i in range(m):
            out = dot(joined_ref[0], weights[i][0], 1, 1 if across else 0)
            for y in range(NY):
                hold[y, i] = out[:, y * LANES : (y + 1) * LANES]
        for k in range(NY):
            at = lax.rem(pos_ref[2] + k, NY)
            for i in range(m):
                outs[k][i, 0] = (hold[at, i] + got_ref[at, i, 0].astype(F32)).astype(BF16)

    ins = [(joined, pl.BlockSpec((1, rows, width), lambda e, pos: (e, 0, 0)))]
    ins += [(w, weight_spec(w, across, False)) for w in mats]
    ins += [
        (got, pl.BlockSpec((NY, m, 1, rows, LANES), lambda e, pos: (0, 0, e, 0, 0))),
    ]
    outs = [
        (sds((m, 2, rows, LANES)), pl.BlockSpec((m, 1, rows, LANES), lambda e, pos: (0, e, 0, 0)))
        for _ in range(NY)
    ]
    scratch = [pltpu.VMEM((NY, m, rows, LANES), F32)]
    return call(body, pos, (2,), ins, outs, scratch, after=after)


def scattered(parts):
    return [parts[0]] + [lax.ppermute(parts[k], "tensor", y_shift(k)) for k in range(1, NY)]


def term_sum(refs, i):
    total = refs[0][i, 0].astype(F32)
    for r in refs[1:]:
        total = total + r[i, 0].astype(F32)
    return total


def sigmoid(v):
    return 1.0 / (1.0 + jnp.exp(-v))


def term_specs(terms):
    m, _, rows, _ = terms[0].shape
    spec = pl.BlockSpec((m, 1, rows, LANES), lambda e, pos: (0, e, 0, 0))
    return [(t, spec) for t in terms]


def activated(pos, terms, after):
    rows = terms[0].shape[2]

    def body(pos_ref, *refs):
        gate, up = term_sum(refs[:NY], 0), term_sum(refs[:NY], 1)
        refs[NY][0, 0] = (gate * sigmoid(gate) * up).astype(BF16)

    outs = [
        (
            sds((2, 1, rows, LANES)),
            pl.BlockSpec((1, 1, rows, LANES), lambda e, pos: (e, 0, 0, 0)),
        )
    ]
    return call(body, pos, (2,), term_specs(terms), outs, after=after)[0]


def differed(pos, terms, hid_terms, after):
    rows = terms[0].shape[2]

    def body(pos_ref, *refs):
        gate, up = term_sum(refs[:NY], 0), term_sum(refs[:NY], 1)
        hid = term_sum(refs[NY : 2 * NY], 0)
        s = sigmoid(gate)
        refs[2 * NY][0, 0] = (hid * up * s * (1.0 + gate * (1.0 - s))).astype(BF16)
        refs[2 * NY][0, 1] = (hid * (gate * s)).astype(BF16)

    outs = [
        (
            sds((2, 2, rows, LANES)),
            pl.BlockSpec((1, 2, rows, LANES), lambda e, pos: (e, 0, 0, 0)),
        )
    ]
    ins = term_specs(terms) + term_specs(hid_terms)
    return call(body, pos, (2,), ins, outs, after=after)[0]


def gathered(own):
    return [own] + [lax.ppermute(own, "tensor", y_shift(k)) for k in range(1, NY)]


def products(pos, mine, others, mats, across, part, after):
    rows = mine[0].shape[2]
    m, hidden = len(mats), 2 * NY * LANES
    width = mats[0].shape[1] if across else mats[0].shape[2]

    def body(pos_ref, *refs):
        ins, other, weights = refs[:NY], refs[NY], refs[NY + 1 : NY + 1 + m]
        outs, fulls = refs[NY + 1 + m], refs[NY + 2 + m :]
        y, c = pos_ref[2], pos_ref[3]
        total = None
        for i in range(m):
            for k in range(NY):
                behind = lax.rem(y + NY - k, NY)
                at = pl.multiple_of((c * NY + behind) * LANES, LANES)
                fulls[i][0, :, pl.ds(at, LANES)] = ins[k][0, i]
                at = pl.multiple_of(((1 - c) * NY + behind) * LANES, LANES)
                fulls[i][0, :, pl.ds(at, LANES)] = other[k, 0, i]
            term = dot(fulls[i][0], weights[i][0], 1, 1 if across else 0)
            total = term if total is None else total + term
        total = total.astype(BF16)
        for k in range(NX):
            outs[k, 0] = total[k * part : (k + 1) * part]

    ins = [(s, pl.BlockSpec((1, m, rows, LANES), lambda e, pos: (e, 0, 0, 0))) for s in mine]
    ins += [(others, pl.BlockSpec((NY, 1, m, rows, LANES), lambda e, pos: (0, e, 0, 0, 0)))]
    ins += [(w, pl.BlockSpec((1,) + w.shape[1:], lambda e, pos: (e, 0, 0))) for w in mats]
    outs = [
        (
            sds((NX, 2, part, width)),
            pl.BlockSpec((NX, 1, part, width), lambda e, pos: (0, e, 0, 0)),
        )
    ]
    outs += [
        (sds((2, rows, hidden)), pl.BlockSpec((1, rows, hidden), lambda e, pos: (e, 0, 0)))
        for _ in range(m)
    ]
    got = call(body, pos, (2,), ins, outs, after=after)
    return got[0], got[1:]


def weight_grad(pos, left, right, left_wide, after):
    rows, a, b = left.shape[1], left.shape[2], right.shape[2]
    ba, bb = (a // 2, b) if left_wide else (a, b // 2)

    def body(pos_ref, left_ref, right_ref, out):
        out[0] = dot(left_ref[0], right_ref[0], 0, 0).astype(BF16)

    def spec(size, cut):
        return pl.BlockSpec((1, rows, size), lambda e, h, pos: (e, 0, h if cut else 0))

    ins = [(left, spec(ba, left_wide)), (right, spec(bb, not left_wide))]
    out = pl.BlockSpec(
        (1, ba, bb), lambda e, h, pos: (e, h if left_wide else 0, 0 if left_wide else h)
    )
    return call(body, pos, (2, 2), ins, [(sds((2, a, b)), out)], after=after)[0]


def exchanged(pieces):
    return lax.all_to_all(pieces, "expert", 0, 0, axis_index_groups=x_groups(), tiled=True)


def ring(own):
    block = {0: own}
    for j in range(1, NZ // 2 + 1):
        block[j] = lax.ppermute(block[j - 1], "expert", z_shift(1))
        if j < NZ // 2:
            block[NZ - j] = lax.ppermute(block[(NZ - j + 1) % NZ], "expert", z_shift(-1))
    return [block[j] for j in range(NZ)]


def returned(values):
    return [values[0]] + [lax.ppermute(values[j], "expert", z_shift(-j)) for j in range(1, NZ)]


def order(value, *after):
    return lax.optimization_barrier((value, after))[0]


def per_device(
    tokens, expert_ids, combine_weight, gate_weight, up_weight, down_weight, out_cotangent
):
    tok_rows, width = tokens.shape
    top_count = expert_ids.shape[1]
    cap = 3 * tok_rows * top_count // (2 * gate_weight.shape[0] * NZ * NX)
    group, share = lax.axis_index("expert"), lax.axis_index("tensor")
    pos = jnp.stack([group // NX, group % NX, share // 2, share % 2]).astype(jnp.int32)

    ids = expert_ids.T
    weight = combine_weight.T
    high = lax.reduce_precision(weight, 8, 7)
    middle = lax.reduce_precision(weight - high, 8, 7)
    low = weight - high - middle
    meta = jnp.concatenate([ids.astype(F32), high, middle, low], axis=1).astype(BF16)
    meta = jnp.pad(meta, ((0, 16 - top_count), (0, width - 4 * tok_rows)))
    part = NZ * cap

    toks = ring(jnp.concatenate([tokens, meta], axis=0))
    cots = ring(out_cotangent)
    far = NZ // 2
    rows = exchanged(dispatch(pos, toks, toks, cap, False, [cots[far], cots[far + 1]]))
    theirs, routed = partial_other(pos, rows, [gate_weight, up_weight], False, [])
    sent = dispatch(pos, toks, cots, cap, True, [theirs])
    parts = partial_own(
        pos, routed, [gate_weight, up_weight], lax.ppermute(theirs, "tensor", flip(1)), False, [sent]
    )
    terms = scattered(parts)
    act = activated(pos, terms, [])
    acts = gathered(act)
    theirs, cotangents = partial_other(pos, exchanged(sent), [down_weight], True, [act])
    parts = partial_own(
        pos, cotangents, [down_weight], lax.ppermute(theirs, "tensor", flip(1)), True, []
    )
    hid_terms = scattered(parts)
    others = lax.ppermute(jnp.stack(order(acts, parts[0])), "tensor", flip(1))
    out, (act_full,) = products(pos, acts, others, [down_weight], False, part, hid_terms[1::2])
    diff = differed(pos, terms, hid_terms, [out])
    diffs = gathered(diff)
    back = exchanged(out)
    down_grad = weight_grad(pos, act_full, cotangents, True, [diff])
    sums = combine(pos, toks, back, cots, cap, [down_grad])
    mixed_parts = returned(sums)
    early = [mixed_parts[j] for j in (1, 2, NZ - 1)]
    others = lax.ppermute(jnp.stack(order(diffs, *early)), "tensor", flip(1))
    out, (gate_full, up_full) = products(
        pos, diffs, others, [gate_weight, up_weight], True, part, [sums[0]]
    )
    back = exchanged(out)
    late = order(mixed_parts, out)
    gate_grad = weight_grad(pos, routed, gate_full, False, [])
    up_grad = weight_grad(pos, routed, up_full, False, [])

    grads = jnp.zeros(ids.shape, F32)
    for j in range(NZ):
        table = late[j][tok_rows : tok_rows + 8, :LANES].astype(F32)
        if j:
            table = table + late[j][tok_rows + 8 :, :LANES].astype(F32)
        for k in range(NX):
            for e in range(2):
                expert = ((pos[0] + j) % NZ * NX + k) * 2 + e
                grads = grads + jnp.where(ids == expert, table[k * 2 + e][None, :], 0.0)
    grads = grads + lax.ppermute(grads, "tensor", flip(1))
    far1, far2, far3 = [lax.ppermute(grads, "tensor", flip(m)) for m in (2, 4, 6)]
    grads = (grads + far1) + (far2 + far3)

    done = [gate_grad, up_grad, grads]
    grad_parts = returned(combine(pos, toks, back, None, cap, done))
    mixed = sum(v[:tok_rows].astype(F32) for v in late).astype(BF16)
    token_grad = sum(v.astype(F32) for v in grad_parts).astype(BF16)
    return (mixed, token_grad, grads.T, gate_grad, up_grad, down_grad)


def solution(mesh):
    placed = (
        P("expert", "tensor"),
        P("expert", None),
        P("expert", None),
        P("expert", "tensor", None),
        P("expert", "tensor", None),
        P("expert", None, "tensor"),
        P("expert", "tensor"),
    )
    return jax.shard_map(
        per_device,
        mesh=mesh,
        in_specs=placed,
        out_specs=(
            P("expert", "tensor"),
            P("expert", "tensor"),
            P("expert", None),
            P("expert", "tensor", None),
            P("expert", "tensor", None),
            P("expert", None, "tensor"),
        ),
        check_vma=False,
    )
```

```python
import jax
import jax.numpy as jnp
from jax import lax
from jax.experimental import pallas as pl
from jax.experimental.pallas import tpu as pltpu
from jax.sharding import PartitionSpec as P

NZ, NX, NY = 8, 4, 4
LANES = 128
F32, BF16 = jnp.float32, jnp.bfloat16


def z_shift(k):
    return [(z * NX + x, (z + k) % NZ * NX + x) for z in range(NZ) for x in range(NX)]


def x_groups():
    return [[z * NX + x for x in range(NX)] for z in range(NZ)]


def y_shift(k):
    return [(y * 2 + c, (y + k) % NY * 2 + c) for y in range(NY) for c in range(2)]


def flip(mask):
    return [(i, i ^ mask) for i in range(NY * 2)]


def call(body, pos, grid, ins, outs, scratch=(), flops=0, after=()):
    first, extra = len(ins), len(after)
    ins = list(ins) + [(a, pl.BlockSpec(memory_space=pl.ANY)) for a in after]
    arrays = [a for a, _ in ins]
    inner = body

    def body(pos_ref, *refs):
        inner(pos_ref, *refs[:first], *refs[first + extra :])

    moved = sum(a.size * a.dtype.itemsize for a in arrays[:first]) + sum(
        s.size * s.dtype.itemsize for s, _ in outs
    )
    return pl.pallas_call(
        body,
        out_shape=[s for s, _ in outs],
        grid_spec=pltpu.PrefetchScalarGridSpec(
            num_scalar_prefetch=1,
            grid=grid,
            in_specs=[s for _, s in ins],
            out_specs=[s for _, s in outs],
            scratch_shapes=list(scratch),
        ),
        compiler_params=pltpu.CompilerParams(vmem_limit_bytes=56 << 20),
        cost_estimate=pl.CostEstimate(flops=1, bytes_accessed=1, transcendentals=0),
    )(pos, *arrays)


def whole(shape):
    return pl.BlockSpec(shape, lambda i, pos: (0,) * len(shape))


def sds(shape, dtype=BF16):
    return jax.ShapeDtypeStruct(shape, dtype)


def dot(a, b, ca, cb):
    return lax.dot_general(a, b, (((ca,), (cb,)), ((), ())), preferred_element_type=F32)


def triangle():
    rows = lax.broadcasted_iota(jnp.int32, (LANES, LANES), 0)
    cols = lax.broadcasted_iota(jnp.int32, (LANES, LANES), 1)
    return jnp.where(rows < cols, 1.0, 0.0).astype(BF16)


def slots(meta, pos, cap):
    ids = meta[:8, :LANES]
    weight = meta[:8, LANES : 2 * LANES] + meta[:8, 2 * LANES : 3 * LANES] + meta[:8, 3 * LANES :]
    named, weights = [], []
    for k in range(NX):
        for e in range(2):
            expert = (pos[0] * NX + k) * 2 + e
            hit = ids == expert.astype(F32)
            named.append(jnp.sum(jnp.where(hit, 1.0, 0.0), axis=0, keepdims=True))
            weights.append(jnp.sum(jnp.where(hit, weight, 0.0), axis=0, keepdims=True))
    all_named = jnp.concatenate(named, axis=0)
    place = dot(all_named.astype(BF16), triangle(), 1, 0)
    place = jnp.where(all_named > 0.5, place, -1.0)
    count = lax.broadcasted_iota(jnp.int32, (cap, LANES), 0).astype(F32)
    tables = [jnp.where(count == place[q : q + 1], 1.0, 0.0) for q in range(2 * NX)]
    return tables, weights


def meta_spec():
    return pl.BlockSpec((16, 4 * LANES), lambda i, pos: (LANES // 16, 0))


def dispatch(pos, metas, blocks, cap, weighted, after=()):
    n, width = len(metas), blocks[0].shape[1]

    def body(pos_ref, *refs):
        p = (pos_ref[0], pos_ref[1])
        rows = []
        for i in range(n):
            tables, weights = slots(refs[i][...].astype(F32), p, cap)
            table = jnp.concatenate(tables, axis=0)
            taken = dot(table.astype(BF16), refs[n + i][0:LANES, :], 1, 0)
            if weighted:
                scale = jnp.concatenate(
                    [jnp.sum(t * w, axis=1, keepdims=True) for t, w in zip(tables, weights)], axis=0
                )
                taken = taken * scale
            rows.append(taken)
        for k in range(NX):
            for e in range(2):
                at = (k * 2 + e) * cap
                refs[2 * n][k, e] = jnp.concatenate(
                    [r[at : at + cap] for r in rows], axis=0
                ).astype(BF16)

    ins = [(m, meta_spec()) for m in metas] + [(b, whole(b.shape)) for b in blocks]
    outs = [(sds((NX, 2, n * cap, width)), whole((NX, 2, n * cap, width)))]
    return call(body, pos, (1,), ins, outs, after=after)[0]


def combine(pos, metas, pieces, cots, cap, after=()):
    n, width = len(metas), pieces.shape[3]
    mixing = cots is not None

    def body(pos_ref, *refs):
        p = (pos_ref[0], pos_ref[1])
        pieces_in = refs[n]
        cots_in = refs[n + 1 : n + 1 + n] if mixing else ()
        outs = refs[len(refs) - n :]
        wide = [[pieces_in[k, e].astype(F32) for e in range(2)] for k in range(NX)]
        for i in range(n):
            tables, weights = slots(refs[i][...].astype(F32), p, cap)
            table = jnp.concatenate(tables, axis=0)
            rows = jnp.concatenate(
                [wide[k][e][i * cap : (i + 1) * cap] for k in range(NX) for e in range(2)], axis=0
            )
            rows16 = rows.astype(BF16)
            if mixing:
                scaled = jnp.concatenate([t * w for t, w in zip(tables, weights)], axis=0)
                high = scaled.astype(BF16)
                low = (scaled - high.astype(F32)).astype(BF16)
                total = dot(high, rows16, 0, 0) + dot(low, rows16, 0, 0)
                picked = dot(table.astype(BF16), cots_in[i][...], 1, 0)
                each = jnp.sum(picked * rows, axis=1, keepdims=True)
                grads = jnp.concatenate(
                    [
                        jnp.sum(t * each[q * cap : (q + 1) * cap], axis=0, keepdims=True)
                        for q, t in enumerate(tables)
                    ]
                    + [jnp.zeros((8 - 2 * NX, LANES), F32)] * (2 * NX < 8),
                    axis=0,
                )
            else:
                total = dot(table.astype(BF16), rows16, 0, 0)
            if i == 0:
                outs[i][0:LANES, :] = total
                if mixing:
                    outs[i][LANES : LANES + 8, 0:LANES] = grads
            else:
                outs[i][0:LANES, :] = total.astype(BF16)
                if mixing:
                    top = grads.astype(BF16)
                    outs[i][LANES : LANES + 16, :] = jnp.zeros((16, width), BF16)
                    outs[i][LANES : LANES + 16, 0:LANES] = jnp.concatenate(
                        [top.astype(F32), grads - top.astype(F32)], axis=0
                    ).astype(BF16)

    ins = [(m, meta_spec()) for m in metas] + [(pieces, whole(pieces.shape))]
    if mixing:
        ins += [(b, whole(b.shape)) for b in cots]
    outs = [sds((LANES + 8 * mixing, width), F32)]
    outs += [sds((LANES + 16 * mixing, width))] * (n - 1)
    outs = [(o, whole(o.shape)) for o in outs]
    return call(body, pos, (1,), ins, outs, after=after)


def weight_spec(w, across, other):
    rows, cols = w.shape[1], w.shape[2]
    half = (lambda pos: 1 - pos[3]) if other else (lambda pos: pos[3])
    if across:
        return pl.BlockSpec((1, rows // 2, cols), lambda e, pos: (e, half(pos), 0))
    return pl.BlockSpec((1, rows, cols // 2), lambda e, pos: (e, 0, half(pos)))


def partial_other(pos, pieces, mats, across, after):
    m, (_, _, part, width) = len(mats), pieces.shape
    rows = NX * part

    def body(pos_ref, *refs):
        rows_in, weights, (theirs, joined) = refs[0], refs[1 : 1 + m], refs[1 + m :]
        left = jnp.concatenate([rows_in[k, 0] for k in range(NX)], axis=0)
        joined[0] = left
        for i in range(m):
            out = dot(left, weights[i][0], 1, 1 if across else 0).astype(BF16)
            for y in range(NY):
                theirs[y, i, 0] = out[:, y * LANES : (y + 1) * LANES]

    ins = [(pieces, pl.BlockSpec((NX, 1, part, width), lambda e, pos: (0, e, 0, 0)))]
    ins += [(w, weight_spec(w, across, True)) for w in mats]
    outs = [
        (
            sds((NY, m, 2, rows, LANES)),
            pl.BlockSpec((NY, m, 1, rows, LANES), lambda e, pos: (0, 0, e, 0, 0)),
        ),
        (sds((2, rows, width)), pl.BlockSpec((1, rows, width), lambda e, pos: (e, 0, 0))),
    ]
    return call(body, pos, (2,), ins, outs, after=after)


def partial_own(pos, joined, mats, got, across, after):
    m, (_, rows, width) = len(mats), joined.shape

    def body(pos_ref, joined_ref, *refs):
        weights, got_ref, outs, hold = refs[:m], refs[m], refs[m + 1 : -1], refs[-1]
        for i in range(m):
            out = dot(joined_ref[0], weights[i][0], 1, 1 if across else 0)
            for y in range(NY):
                hold[y, i] = out[:, y * LANES : (y + 1) * LANES]
        for k in range(NY):
            at = lax.rem(pos_ref[2] + k, NY)
            for i in range(m):
                outs[k][i, 0] = (hold[at, i] + got_ref[at, i, 0].astype(F32)).astype(BF16)

    ins = [(joined, pl.BlockSpec((1, rows, width), lambda e, pos: (e, 0, 0)))]
    ins += [(w, weight_spec(w, across, False)) for w in mats]
    ins += [
        (got, pl.BlockSpec((NY, m, 1, rows, LANES), lambda e, pos: (0, 0, e, 0, 0))),
    ]
    outs = [
        (sds((m, 2, rows, LANES)), pl.BlockSpec((m, 1, rows, LANES), lambda e, pos: (0, e, 0, 0)))
        for _ in range(NY)
    ]
    scratch = [pltpu.VMEM((NY, m, rows, LANES), F32)]
    return call(body, pos, (2,), ins, outs, scratch, after=after)


def scattered(parts):
    return [parts[0]] + [lax.ppermute(parts[k], "tensor", y_shift(k)) for k in range(1, NY)]


def term_sum(refs, i):
    total = refs[0][i, 0].astype(F32)
    for r in refs[1:]:
        total = total + r[i, 0].astype(F32)
    return total


def sigmoid(v):
    return 1.0 / (1.0 + jnp.exp(-v))


def term_specs(terms):
    m, _, rows, _ = terms[0].shape
    spec = pl.BlockSpec((m, 1, rows, LANES), lambda e, pos: (0, e, 0, 0))
    return [(t, spec) for t in terms]


def activated(pos, terms, after):
    rows = terms[0].shape[2]

    def body(pos_ref, *refs):
        gate, up = term_sum(refs[:NY], 0), term_sum(refs[:NY], 1)
        refs[NY][0, 0] = (gate * sigmoid(gate) * up).astype(BF16)

    outs = [
        (
            sds((2, 1, rows, LANES)),
            pl.BlockSpec((1, 1, rows, LANES), lambda e, pos: (e, 0, 0, 0)),
        )
    ]
    return call(body, pos, (2,), term_specs(terms), outs, after=after)[0]


def differed(pos, terms, hid_terms, after):
    rows = terms[0].shape[2]

    def body(pos_ref, *refs):
        gate, up = term_sum(refs[:NY], 0), term_sum(refs[:NY], 1)
        hid = term_sum(refs[NY : 2 * NY], 0)
        s = sigmoid(gate)
        refs[2 * NY][0, 0] = (hid * up * s * (1.0 + gate * (1.0 - s))).astype(BF16)
        refs[2 * NY][0, 1] = (hid * (gate * s)).astype(BF16)

    outs = [
        (
            sds((2, 2, rows, LANES)),
            pl.BlockSpec((1, 2, rows, LANES), lambda e, pos: (e, 0, 0, 0)),
        )
    ]
    ins = term_specs(terms) + term_specs(hid_terms)
    return call(body, pos, (2,), ins, outs, after=after)[0]


def gathered(own):
    return [own] + [lax.ppermute(own, "tensor", y_shift(k)) for k in range(1, NY)]


def products(pos, mine, others, mats, across, part, after):
    rows = mine[0].shape[2]
    m, hidden = len(mats), 2 * NY * LANES
    width = mats[0].shape[1] if across else mats[0].shape[2]

    def body(pos_ref, *refs):
        ins, other, weights = refs[:NY], refs[NY], refs[NY + 1 : NY + 1 + m]
        outs, fulls = refs[NY + 1 + m], refs[NY + 2 + m :]
        y, c = pos_ref[2], pos_ref[3]
        total = None
        for i in range(m):
            for k in range(NY):
                behind = lax.rem(y + NY - k, NY)
                at = pl.multiple_of((c * NY + behind) * LANES, LANES)
                fulls[i][0, :, pl.ds(at, LANES)] = ins[k][0, i]
                at = pl.multiple_of(((1 - c) * NY + behind) * LANES, LANES)
                fulls[i][0, :, pl.ds(at, LANES)] = other[k, 0, i]
            term = dot(fulls[i][0], weights[i][0], 1, 1 if across else 0)
            total = term if total is None else total + term
        total = total.astype(BF16)
        for k in range(NX):
            outs[k, 0] = total[k * part : (k + 1) * part]

    ins = [(s, pl.BlockSpec((1, m, rows, LANES), lambda e, pos: (e, 0, 0, 0))) for s in mine]
    ins += [(others, pl.BlockSpec((NY, 1, m, rows, LANES), lambda e, pos: (0, e, 0, 0, 0)))]
    ins += [(w, pl.BlockSpec((1,) + w.shape[1:], lambda e, pos: (e, 0, 0))) for w in mats]
    outs = [
        (
            sds((NX, 2, part, width)),
            pl.BlockSpec((NX, 1, part, width), lambda e, pos: (0, e, 0, 0)),
        )
    ]
    outs += [
        (sds((2, rows, hidden)), pl.BlockSpec((1, rows, hidden), lambda e, pos: (e, 0, 0)))
        for _ in range(m)
    ]
    got = call(body, pos, (2,), ins, outs, after=after)
    return got[0], got[1:]


def weight_grad(pos, left, right, left_wide, after):
    rows, a, b = left.shape[1], left.shape[2], right.shape[2]
    ba, bb = (a // 2, b) if left_wide else (a, b // 2)

    def body(pos_ref, left_ref, right_ref, out):
        out[0] = dot(left_ref[0], right_ref[0], 0, 0).astype(BF16)

    def spec(size, cut):
        return pl.BlockSpec((1, rows, size), lambda e, h, pos: (e, 0, h if cut else 0))

    ins = [(left, spec(ba, left_wide)), (right, spec(bb, not left_wide))]
    out = pl.BlockSpec(
        (1, ba, bb), lambda e, h, pos: (e, h if left_wide else 0, 0 if left_wide else h)
    )
    return call(body, pos, (2, 2), ins, [(sds((2, a, b)), out)], after=after)[0]


def exchanged(pieces):
    return lax.all_to_all(pieces, "expert", 0, 0, axis_index_groups=x_groups(), tiled=True)


def ring(own):
    block = {0: own}
    for j in range(1, NZ // 2 + 1):
        block[j] = lax.ppermute(block[j - 1], "expert", z_shift(1))
        if j < NZ // 2:
            block[NZ - j] = lax.ppermute(block[(NZ - j + 1) % NZ], "expert", z_shift(-1))
    return [block[j] for j in range(NZ)]


def returned(values):
    return [values[0]] + [lax.ppermute(values[j], "expert", z_shift(-j)) for j in range(1, NZ)]


def order(value, *after):
    return lax.optimization_barrier((value, after))[0]


def per_device(
    tokens, expert_ids, combine_weight, gate_weight, up_weight, down_weight, out_cotangent
):
    tok_rows, width = tokens.shape
    top_count = expert_ids.shape[1]
    cap = 3 * tok_rows * top_count // (2 * gate_weight.shape[0] * NZ * NX)
    group, share = lax.axis_index("expert"), lax.axis_index("tensor")
    pos = jnp.stack([group // NX, group % NX, share // 2, share % 2]).astype(jnp.int32)

    ids = expert_ids.T
    weight = combine_weight.T
    high = lax.reduce_precision(weight, 8, 7)
    middle = lax.reduce_precision(weight - high, 8, 7)
    low = weight - high - middle
    meta = jnp.concatenate([ids.astype(F32), high, middle, low], axis=1).astype(BF16)
    meta = jnp.pad(meta, ((0, 16 - top_count), (0, width - 4 * tok_rows)))
    part = NZ * cap

    toks = ring(jnp.concatenate([tokens, meta], axis=0))
    cots = ring(out_cotangent)
    far = NZ // 2
    rows = exchanged(dispatch(pos, toks, toks, cap, False, [cots[far], cots[far + 1]]))
    theirs, routed = partial_other(pos, rows, [gate_weight, up_weight], False, [])
    sent = dispatch(pos, toks, cots, cap, True, [theirs])
    parts = partial_own(
        pos, routed, [gate_weight, up_weight], lax.ppermute(theirs, "tensor", flip(1)), False, [sent]
    )
    terms = scattered(parts)
    act = activated(pos, terms, [])
    acts = gathered(act)
    theirs, cotangents = partial_other(pos, exchanged(sent), [down_weight], True, [act])
    parts = partial_own(
        pos, cotangents, [down_weight], lax.ppermute(theirs, "tensor", flip(1)), True, []
    )
    hid_terms = scattered(parts)
    others = lax.ppermute(jnp.stack(acts), "tensor", flip(1))
    out, (act_full,) = products(pos, acts, others, [down_weight], False, part, [parts[0]])
    diff = differed(pos, terms, hid_terms, [out])
    diffs = gathered(diff)
    back = exchanged(out)
    down_grad = weight_grad(pos, act_full, cotangents, True, [diff])
    sums = combine(pos, toks, back, cots, cap, [down_grad])
    mixed_parts = returned(sums)
    early = [mixed_parts[j] for j in (1, 2, NZ - 1)]
    others = lax.ppermute(jnp.stack(order(diffs, *early)), "tensor", flip(1))
    out, (gate_full, up_full) = products(
        pos, diffs, others, [gate_weight, up_weight], True, part, [sums[0]]
    )
    back = exchanged(out)
    late = order(mixed_parts, out)
    gate_grad = weight_grad(pos, routed, gate_full, False, [])
    up_grad = weight_grad(pos, routed, up_full, False, [])

    grads = jnp.zeros(ids.shape, F32)
    for j in range(NZ):
        table = late[j][tok_rows : tok_rows + 8, :LANES].astype(F32)
        if j:
            table = table + late[j][tok_rows + 8 :, :LANES].astype(F32)
        for k in range(NX):
            for e in range(2):
                expert = ((pos[0] + j) % NZ * NX + k) * 2 + e
                grads = grads + jnp.where(ids == expert, table[k * 2 + e][None, :], 0.0)
    grads = grads + lax.ppermute(grads, "tensor", flip(1))
    far1, far2, far3 = [lax.ppermute(grads, "tensor", flip(m)) for m in (2, 4, 6)]
    grads = (grads + far1) + (far2 + far3)

    done = [gate_grad, up_grad, grads]
    grad_parts = returned(combine(pos, toks, back, None, cap, done))
    mixed = sum(v[:tok_rows].astype(F32) for v in late).astype(BF16)
    token_grad = sum(v.astype(F32) for v in grad_parts).astype(BF16)
    return (mixed, token_grad, grads.T, gate_grad, up_grad, down_grad)


def solution(mesh):
    placed = (
        P("expert", "tensor"),
        P("expert", None),
        P("expert", None),
        P("expert", "tensor", None),
        P("expert", "tensor", None),
        P("expert", None, "tensor"),
        P("expert", "tensor"),
    )
    return jax.shard_map(
        per_device,
        mesh=mesh,
        in_specs=placed,
        out_specs=(
            P("expert", "tensor"),
            P("expert", "tensor"),
            P("expert", None),
            P("expert", "tensor", None),
            P("expert", "tensor", None),
            P("expert", None, "tensor"),
        ),
        check_vma=False,
    )
```
